512 devices in a mesh: row: 16 (over y, z_hi, core), col: 32 (over x, z_lo).
Axes of the slice: x: 4, y: 4, z: 16 (z_hi: 2, z_lo: 8; z = z_hi * 8 + z_lo), core: 2. Of those that a mesh axis runs over, the one named last changes fastest.
Arguments:
- embedding: bfloat16 [2048, 128], P('row'), may hold values from -6 to 6
- kernel: bfloat16 [3, 3, 64, 64], replicated, may hold values from -0.25 to 0.25
- cotangent: bfloat16 [2048, 2048, 64], P('row', 'col'), may hold values from -6 to 6
Outputs:
- prediction: float32 [2048, 2048, 64], P('row', 'col')
- grad_kernel: float32 [3, 3, 64, 64], replicated
- grad_embedding: float32 [2048, 128], P('row')
The draws below stay inside these ranges and needn't reach their ends.
All inputs are finite; a program needn't handle non-finite values.
Results may differ from the reference program's by a relative error of at most 0.0031.
Values may be sent and summed in bfloat16 or wider, within the bound.
No kernel may reach another device: no remote copies, remote signals or barrier semaphores. Data moves between devices by JAX's collectives and lax.ppermute only.
A program may use at most 128 MiB of HBM per device.

```python
import jax
import jax.numpy as jnp
from jax import lax

PAIR_CHANNELS = 64
DILATION_STEP = 8
REGION_BINS = 2048
DEVICE_ROW_BINS = 128
N_ROW = 16


def shard_levels(key, shape, pieces, smallest, largest):
    gain, own = 1.0, jax.random.fold_in(key, 6)
    for dim, parts in pieces:
        steps = jnp.exp(jax.random.uniform(jax.random.fold_in(own, dim), (parts,), jnp.float32, smallest / len(pieces), largest / len(pieces)))
        gain = gain * jnp.repeat(steps, shape[dim] // parts).reshape([-1 if axis == dim else 1 for axis in range(len(shape))])
    return gain


def bell_draw(own_key, extent, deviation, bound, split=(), kind=jnp.bfloat16):
    level = shard_levels(own_key, extent, split, -0.22, 0.18) if split else 1.0
    drawn = jax.random.normal(own_key, extent, jnp.float32) * deviation * level
    return jnp.minimum(jnp.maximum(drawn, -bound), bound).astype(kind)


def setup_inputs(seed: int = 0) -> dict:
    seeds = jax.random.split(jax.random.key(seed), 4)
    embedding = bell_draw(seeds[0], (REGION_BINS, 2 * PAIR_CHANNELS), 1.0, 6.0, ((0, 16),))
    kernel = bell_draw(seeds[1], (3, 3, PAIR_CHANNELS, PAIR_CHANNELS), (9 * PAIR_CHANNELS) ** -0.5, 0.25)
    cotangent = bell_draw(seeds[2], (REGION_BINS, REGION_BINS, PAIR_CHANNELS), 1.0, 6.0, ((0, 16), (1, 32)))
    return {"embedding": embedding, "kernel": kernel, "cotangent": cotangent}


def reference(embedding, kernel, cotangent):
    whole_region = embedding.astype(jnp.float32)
    embedding_padded = jnp.pad(whole_region, ((DILATION_STEP, DILATION_STEP), (0, 0)))
    inside_mask = jnp.pad(jnp.ones((REGION_BINS,), jnp.float32), (DILATION_STEP, DILATION_STEP))
    col_mult = embedding_padded[:, :PAIR_CHANNELS]
    col_add = embedding_padded[:, PAIR_CHANNELS:]
    cotangent_padded = jnp.pad(cotangent, ((DILATION_STEP, DILATION_STEP), (DILATION_STEP, DILATION_STEP), (0, 0)))
    weights = kernel.astype(jnp.float32)

    def block(totals, block_index):
        kernel_acc, col_acc = totals
        row_offset = block_index.astype(jnp.int32) * DEVICE_ROW_BINS
        row_embedding = lax.dynamic_slice_in_dim(embedding_padded, row_offset, DEVICE_ROW_BINS + 2 * DILATION_STEP, 0)
        row_inside_mask = lax.dynamic_slice_in_dim(inside_mask, row_offset, DEVICE_ROW_BINS + 2 * DILATION_STEP, 0)
        preactivation_wide = row_embedding[:, None, :PAIR_CHANNELS] * col_mult[None] + row_embedding[:, None, PAIR_CHANNELS:] + col_add[None]
        mask = row_inside_mask[:, None, None] * inside_mask[None, :, None]
        activation_wide = (jax.nn.silu(preactivation_wide) * mask).astype(jnp.bfloat16).astype(jnp.float32)
        cotangent_wide = lax.dynamic_slice_in_dim(cotangent_padded, row_offset, DEVICE_ROW_BINS + 2 * DILATION_STEP, 0).astype(jnp.float32)
        cotangent_local = cotangent_wide[DILATION_STEP:DILATION_STEP + DEVICE_ROW_BINS, DILATION_STEP:DILATION_STEP + REGION_BINS]
        forward = jnp.zeros((DEVICE_ROW_BINS, REGION_BINS, PAIR_CHANNELS), jnp.float32)
        backward = jnp.zeros((DEVICE_ROW_BINS, REGION_BINS, PAIR_CHANNELS), jnp.float32)
        kernel_rows = []
        for kernel_tap_row in range(3):
            kernel_cols = []
            for kernel_tap_column in range(3):
                shifted_pairs = activation_wide[kernel_tap_row * DILATION_STEP:kernel_tap_row * DILATION_STEP + DEVICE_ROW_BINS, kernel_tap_column * DILATION_STEP:kernel_tap_column * DILATION_STEP + REGION_BINS]
                forward = forward + jnp.einsum('ijc,cd->ijd', shifted_pairs, weights[kernel_tap_row, kernel_tap_column])
                kernel_cols.append(jnp.einsum('ijc,ijd->cd', shifted_pairs, cotangent_local))
                cotangent_shifted = cotangent_wide[(2 - kernel_tap_row) * DILATION_STEP:(2 - kernel_tap_row) * DILATION_STEP + DEVICE_ROW_BINS, (2 - kernel_tap_column) * DILATION_STEP:(2 - kernel_tap_column) * DILATION_STEP + REGION_BINS]
                backward = backward + jnp.einsum('ijd,cd->ijc', cotangent_shifted, weights[kernel_tap_row, kernel_tap_column])
            kernel_rows.append(jnp.stack(kernel_cols))
        kernel_acc = kernel_acc + jnp.stack(kernel_rows)
        preactivation = preactivation_wide[DILATION_STEP:DILATION_STEP + DEVICE_ROW_BINS, DILATION_STEP:DILATION_STEP + REGION_BINS]
        sigmoid_val = jax.nn.sigmoid(preactivation)
        grad_pre = backward * sigmoid_val * (1.0 + preactivation * (1.0 - sigmoid_val))
        row_multiplier = row_embedding[DILATION_STEP:DILATION_STEP + DEVICE_ROW_BINS, :PAIR_CHANNELS]
        col_real = whole_region[:, :PAIR_CHANNELS]
        row_part = jnp.concatenate([jnp.sum(grad_pre * col_real[None], axis=1), jnp.sum(grad_pre, axis=1)], axis=1)
        col_part = jnp.concatenate([jnp.sum(grad_pre * row_multiplier[:, None], axis=0), jnp.sum(grad_pre, axis=0)], axis=1)
        return (kernel_acc, col_acc + col_part), (forward, row_part)

    start_totals = (jnp.zeros((3, 3, PAIR_CHANNELS, PAIR_CHANNELS), jnp.float32), jnp.zeros((REGION_BINS, 2 * PAIR_CHANNELS), jnp.float32))
    totals, stacked = lax.scan(block, start_totals, jnp.arange(N_ROW))
    kernel_acc, col_acc = totals
    forwards, row_parts = stacked
    prediction = forwards.reshape(REGION_BINS, REGION_BINS, PAIR_CHANNELS)
    grad_kernel = kernel_acc / REGION_BINS
    grad_embedding = (row_parts.reshape(REGION_BINS, 2 * PAIR_CHANNELS) + col_acc) * (REGION_BINS ** -0.5)
    return prediction, grad_kernel, grad_embedding
```

```python
import jax
import jax.numpy as jnp
from jax import lax
from jax.experimental import pallas as pl
from jax.experimental.pallas import tpu as pltpu
from jax.sharding import PartitionSpec as P

BF16 = jnp.bfloat16
F32 = jnp.float32

ROWS, COLS = 16, 32


def device_id(y, z_hi, core, x, z_lo):
    return (y * 4 + z_hi * 2 + core) * COLS + x * 8 + z_lo


PLANE_GROUPS = [
    [device_id(y, zh, k, x, zl) for y in range(4) for k in range(2) for x in range(4)]
    for zh in range(2)
    for zl in range(8)
]
LINE_GROUPS = [
    [device_id(y, zh, k, x, zl) for zh in range(2) for zl in range(8)]
    for y in range(4)
    for k in range(2)
    for x in range(4)
]
ROW_GROUPS = [
    [
        device_id(r // 4, r // 2 % 2, r % 2, x, (zl + 4 * (r // 2 % 2)) % 8)
        for r in range(ROWS)
    ]
    for x in range(4)
    for zl in range(8)
]


def exchange(parts, groups):
    return lax.all_to_all(parts, ("row", "col"), 0, 0, axis_index_groups=groups)


C = 64
I = 128
J = 64
G = 8


def lanes():
    return lax.broadcasted_iota(jnp.int32, (C, I), 1)


def turn(x, shift):
    return pltpu.roll(x.astype(F32), shift % I, 1).astype(x.dtype)


def dot(a, b):
    return lax.dot_general(a, b, (((1,), (0,)), ((), ())), preferred_element_type=F32)


def dot_lanes(a, b):
    return lax.dot_general(a, b, (((1,), (1,)), ((), ())), preferred_element_type=F32)


def split_dot(x, picks):
    high = x.astype(BF16)
    low = (x - high.astype(F32)).astype(BF16)
    return dot(high, picks) + dot(low, picks)


def shifted(act, edge, jj, lane):
    ends = turn(edge, -(16 * jj + 8))
    wide = act.astype(F32)
    before = jnp.where(lane < 8, ends.astype(F32), pltpu.roll(wide, 8, 1)).astype(BF16)
    after = jnp.where(lane >= 120, ends.astype(F32), pltpu.roll(wide, I - 8, 1)).astype(BF16)
    return jnp.concatenate([before, act, after], axis=0)


def main_kernel(cot, w, row_wide, col_wide, ids, out, act_out, edge_out, ga, gae, gk, acc):
    lane = lanes()
    slot = lane % 16
    weights = jnp.concatenate(
        [jnp.concatenate([w[3 * a + b] for a in range(3)], axis=1) for b in range(3)], axis=0
    )
    edge_weights = jnp.concatenate(
        [jnp.concatenate([w[b], w[6 + b]], axis=1) for b in range(3)], axis=0
    )

    def put(ref, place, value, fresh):
        ref[place] = value if fresh else ref[place] + value

    def back(k, first):
        fresh = [first, first, True]
        packed = jnp.zeros((C, I), F32)
        for p in range(0, G, 2):
            stacks = []
            for q in (p, p + 1):
                x = cot[G * k + q]
                wide = x.astype(F32)
                later = jnp.where(lane < 120, pltpu.roll(wide, I - 8, 1), 0.0).astype(BF16)
                earlier = jnp.where(lane >= 8, pltpu.roll(wide, 8, 1), 0.0).astype(BF16)
                stacks.append(jnp.concatenate([later, x, earlier], axis=0))
                packed = jnp.where(lane // 16 == q, pltpu.roll(wide, (16 * q + 8) % I, 1), packed)
            part = dot(weights, jnp.concatenate(stacks, axis=1))
            for b in range(3):
                for n, q in enumerate((p, p + 1)):
                    value = part[C * b : C * b + C, I * n : I * n + I]
                    put(ga, G * (k + b) + q, value, fresh[b])
        both = jnp.concatenate(
            [jnp.where(slot >= 8, packed, 0.0), jnp.where(slot < 8, packed, 0.0)], axis=0
        ).astype(BF16)
        part = dot(edge_weights, both)
        for b in range(3):
            put(gae, k + b, part[C * b : C * b + C], fresh[b])

    back(0, True)

    @pl.loop(1, 8)
    def _(k):
        back(k, False)

    acc[...] = jnp.zeros_like(acc)
    gk[...] = jnp.zeros_like(gk)
    wide = row_wide[...].astype(F32)
    row = wide[G : G + I].T
    ends = jnp.concatenate([wide[G + I :], wide[:G]], axis=0)
    edge_row = jnp.concatenate([ends] * 8, axis=0).T
    u_row, v_row = row[:C], row[C:]
    u_edge, v_edge = edge_row[:C], edge_row[C:]
    col_f = col_wide[...].astype(F32).T
    col = col_f.astype(BF16)
    has_low = (ids[0] > 0).astype(F32)
    has_high = (ids[0] < ROWS - 1).astype(F32)
    edge_mask = jnp.where(slot < 8, has_high, has_low)
    m0 = lax.broadcasted_iota(jnp.int32, (I, I), 0)
    m1 = lax.broadcasted_iota(jnp.int32, (I, I), 1)

    def gate(x):
        s = 0.5 + 0.5 * jnp.tanh(0.5 * x)
        y = x * s
        return y, s + y * (1.0 - s)

    def group(k, taps, mask):
        spread = (m0 == G * k + m1 // 16).astype(BF16)
        gather = (m1 == G * k + m0 // 16).astype(BF16)
        here = dot(col, spread)
        edge_on = edge_mask * mask
        y, slope = gate(u_edge * here[:C] + (v_edge + here[C:]))
        edge_act = y * edge_on
        edge_out[k] = edge_act.astype(BF16)
        g = gae[k] * (slope * edge_on)
        acc[4] += g * here[:C]
        acc[5] += g
        acc[2] += split_dot(g * u_edge, gather)
        acc[3] += split_dot(g, gather)
        near = pltpu.roll(col_f, (I - G * k) % I, 1)
        stacks = []
        for q in range(G):
            uc, vc = near[:C, q : q + 1], near[C:, q : q + 1]
            y, slope = gate(u_row * uc + (v_row + vc))
            act = (y * mask).astype(BF16)
            act_out[G * k + q] = act
            stacks.append(shifted(act, edge_act, q, lane))
            g = ga[G * k + q] * (slope * mask)
            acc[0] += g * uc
            acc[1] += g
            here_lane = lane == G * k + q
            acc[2] += jnp.where(here_lane, jnp.sum(g * u_row, axis=1, keepdims=True), 0.0)
            acc[3] += jnp.where(here_lane, jnp.sum(g, axis=1, keepdims=True), 0.0)
        acts = jnp.concatenate(stacks, axis=1)
        cots = jnp.concatenate(
            [jnp.concatenate([cot[G * (k - b) + q] for q in range(G)], axis=1) for b in taps], axis=0
        )
        gk[:, C * taps[0] : C * (taps[-1] + 1)] += dot_lanes(acts, cots)

    group(0, [0], (ids[1] > 0).astype(F32))
    group(1, [0, 1], 1.0)

    @pl.loop(2, 8)
    def _(k):
        group(k, [0, 1, 2], 1.0)

    group(8, [1, 2], 1.0)
    group(9, [2], (ids[1] < COLS - 1).astype(F32))

    def fold(x):
        x = x + pltpu.roll(x, 64, 1)
        x = x + pltpu.roll(x, 32, 1)
        return x + pltpu.roll(x, 16, 1)

    big_lane = lax.broadcasted_iota(jnp.int32, (2 * C, I), 1)
    ends = pltpu.roll(fold(jnp.concatenate([acc[4], acc[5]], axis=0)), 80, 1)
    sums = jnp.concatenate([acc[2], acc[3]], axis=0)
    total = gk[...]
    rest = jnp.concatenate([total[: 2 * C, 128:160]] * 4, axis=1)
    misc = jnp.where(big_lane < 80, sums, jnp.where(big_lane < 96, ends, rest))
    tail = jnp.concatenate([total[128:, 128:], total[:64, 160:], total[64:128, 160:]], axis=1)
    rows = jnp.concatenate([acc[0], acc[1]], axis=0)
    for t in range(32):
        if t < 24:
            out[t, :8] = total[8 * t : 8 * t + 8, :128]
        else:
            out[t, :8] = tail[8 * (t - 24) : 8 * (t - 24) + 8]
        out[t, 8:12] = rows[4 * t : 4 * t + 4]
        out[t, 12:16] = misc[4 * t : 4 * t + 4]


def whole(shape, dtype):
    return jax.ShapeDtypeStruct(shape, dtype)


VMEM = pl.BlockSpec(memory_space=pltpu.VMEM)
SMEM = pl.BlockSpec(memory_space=pltpu.SMEM)


def run_main(cot, w, row_wide, col_wide, ids):
    return pl.pallas_call(
        main_kernel,
        out_shape=(whole((32, 16, I), F32), whole((80, C, I), BF16), whole((10, C, I), BF16)),
        in_specs=[VMEM] * 4 + [SMEM],
        out_specs=(VMEM, VMEM, VMEM),
        scratch_shapes=[
            pltpu.VMEM((80, C, I), F32),
            pltpu.VMEM((10, C, I), F32),
            pltpu.VMEM((192, 192), F32),
            pltpu.VMEM((6, C, I), F32),
        ],
        compiler_params=pltpu.CompilerParams(vmem_limit_bytes=40 * 2**20),
        cost_estimate=pl.CostEstimate(flops=1_300_000_000, bytes_accessed=3_500_000, transcendentals=700_000),
        name="tile_gradients",
    )(cot, w, row_wide, col_wide, ids)


def forward_kernel(act, edge, w, out):
    lane = lanes()
    weights = w[...]

    def group(k, taps):
        edge_act = edge[k].astype(F32)
        for p in range(0, G, 2):
            stack = jnp.concatenate(
                [shifted(act[G * k + q], edge_act, q, lane) for q in (p, p + 1)], axis=1
            )
            part = dot(weights[C * taps[0] : C * (taps[-1] + 1)], stack)
            for n, b in enumerate(taps):
                for h, q in enumerate((p, p + 1)):
                    value = part[C * n : C * n + C, I * h : I * h + I]
                    place = G * (k - b) + q
                    out[place] = value if b == 0 else out[place] + value

    group(0, [0])
    group(1, [0, 1])

    @pl.loop(2, 8)
    def _(k):
        group(k, [0, 1, 2])

    group(8, [1, 2])
    group(9, [2])


def run_forward(act, edge, w):
    return pl.pallas_call(
        forward_kernel,
        out_shape=whole((J, C, I), F32),
        in_specs=[VMEM] * 3,
        out_specs=VMEM,
        compiler_params=pltpu.CompilerParams(vmem_limit_bytes=40 * 2**20),
        cost_estimate=pl.CostEstimate(flops=700_000_000, bytes_accessed=3_500_000, transcendentals=0),
        name="tile_forward",
    )(act, edge, w)


def reduce_all(parts, z_hi):
    got = exchange(parts, PLANE_GROUPS)
    kernel_sum = jnp.sum(got[:, :8], axis=0)
    rest_sum = jnp.sum(got[:, 12:, 96:], axis=0)
    by_row = got.reshape(8, 4, 16, 128)
    row_main = jnp.sum(by_row[:, :, 8:12], axis=1).reshape(32, 128)
    row_edge = jnp.sum(by_row[:, :, 12:, 80:96], axis=1).reshape(32, 16)
    col_wide = jnp.sum(by_row[:, :, 12:, :80], axis=0).reshape(16, 80)
    tail = jnp.concatenate(
        [col_wide, row_edge[:16], row_edge[16:], rest_sum.reshape(16, 8), jnp.zeros((16, 8), F32)], axis=1
    )
    share = jnp.concatenate([kernel_sum, row_main, tail], axis=0).astype(BF16)
    got = exchange(jnp.broadcast_to(share[None], (16, 56, 128)), LINE_GROUPS).astype(F32)
    kernel_sum = jnp.sum(got[:, :8], axis=0)
    rest_sum = jnp.sum(got[:, 40:, 112:120], axis=0).reshape(4, 32)
    halves = got.reshape(2, 8, 56, 128)
    mine = lax.dynamic_index_in_dim(halves, z_hi, 0, keepdims=False)
    total = jnp.sum(mine[:, 8:40], axis=0).reshape(4, 2, 4, 128)
    edges = jnp.sum(halves[:, :, 40:, 80:112], axis=1)
    edges = jnp.concatenate([edges[:, :, :16], edges[:, :, 16:]], axis=1).reshape(2, 4, 2, 4, 16)
    edges = edges.transpose(1, 0, 2, 3, 4).reshape(16, 4, 16)
    none = jnp.zeros((1, 4, 8), F32)
    from_left = jnp.concatenate([none, edges[:-1, :, :8]], axis=0)
    from_right = jnp.concatenate([edges[1:, :, 8:], none], axis=0)
    cols = jnp.sum(halves[:, :, 40:, :80], axis=0).reshape(8, 4, 4, 80)
    cols = cols.transpose(1, 0, 2, 3).reshape(32, 4, 80)
    low = jnp.concatenate([none, cols[:-1, :, 72:]], axis=0)
    high = jnp.concatenate([cols[1:, :, :8], none], axis=0)
    inner = cols[:, :, 8:72]
    inner = jnp.concatenate([inner[:, :, :8] + low, inner[:, :, 8:56], inner[:, :, 56:] + high], axis=2)
    inner = inner.reshape(16, 2, 4, 64).transpose(0, 2, 1, 3).reshape(16, 4, 128)
    inner = jnp.concatenate(
        [inner[:, :, :8] + from_left, inner[:, :, 8:120], inner[:, :, 120:] + from_right], axis=2
    )
    inner = lax.dynamic_index_in_dim(inner.reshape(4, 2, 2, 4, 128), z_hi, 1, keepdims=False)
    total = (total + inner).reshape(8, 1, 4, 128)
    total = jnp.broadcast_to(total, (8, 4, 4, 128)).reshape(32, 4, 128)
    rest_sum = jnp.pad(rest_sum, ((0, 0), (0, 96)))
    done = jnp.concatenate([kernel_sum, rest_sum], axis=0)
    done = jnp.broadcast_to(done[None], (32, 12, 128))
    got = exchange(jnp.concatenate([done, total], axis=1), PLANE_GROUPS)
    main = got[:, :8].reshape(256, 128)
    rest = got[:, 8:12, :32].reshape(128, 32)
    right = jnp.concatenate([rest, jnp.concatenate([main[192:, 64:96], main[192:, 96:]], axis=0)], axis=1)
    right = jnp.concatenate([right, main[192:, :64]], axis=0)
    gk = jnp.concatenate([main[:192], right], axis=1)
    return gk, got[:, 12:].reshape(128, 128)


def on_device(embedding, kernel, cotangent):
    rows_local = embedding.shape[0]
    bin_count = rows_local * ROWS
    row_id = lax.axis_index("row")
    col_id = lax.axis_index("col")
    everyone = exchange(jnp.broadcast_to(embedding[None], (ROWS,) + embedding.shape), ROW_GROUPS)
    everyone = jnp.pad(everyone.reshape(bin_count, 2 * C), ((G, I), (0, 0)))
    row_wide = lax.dynamic_slice_in_dim(everyone, row_id * rows_local, rows_local + 2 * G, 0)
    col_wide = lax.dynamic_slice_in_dim(everyone, col_id * J, I, 0)
    ids = jnp.stack([row_id, col_id])
    parts, act, edge = run_main(
        cotangent.transpose(1, 2, 0), kernel.reshape(9, C, C), row_wide, col_wide, ids
    )
    taps = kernel.transpose(1, 3, 0, 2).reshape(192, 192)
    prediction = run_forward(act, edge, taps).transpose(2, 0, 1)
    gk, ge = reduce_all(parts, row_id // 2 % 2)
    gk = gk.reshape(3, C, 3, C).transpose(0, 2, 1, 3)
    return prediction, gk / bin_count, ge.T * float(bin_count) ** (-0.5)


def solution(mesh):
    in_specs = (P("row", None), P(), P("row", "col", None))
    out_specs = (P("row", "col", None), P(), P("row", None))
    return jax.shard_map(
        on_device, mesh=mesh, in_specs=in_specs, out_specs=out_specs, check_vma=False
    )
```

```python
import jax
import jax.numpy as jnp
from jax import lax
from jax.experimental import pallas as pl
from jax.experimental.pallas import tpu as pltpu
from jax.sharding import PartitionSpec as P

BF16 = jnp.bfloat16
F32 = jnp.float32

ROWS, COLS = 16, 32


def device_id(y, z_hi, core, x, z_lo):
    return (y * 4 + z_hi * 2 + core) * COLS + x * 8 + z_lo


PLANE_GROUPS = [
    [device_id(y, zh, k, x, zl) for y in range(4) for k in range(2) for x in range(4)]
    for zh in range(2)
    for zl in range(8)
]
LINE_GROUPS = [
    [device_id(y, zh, k, x, zl) for zh in range(2) for zl in range(8)]
    for y in range(4)
    for k in range(2)
    for x in range(4)
]
ROW_GROUPS = [
    [
        device_id(r // 4, r // 2 % 2, r % 2, x, (zl + 4 * (r // 2 % 2)) % 8)
        for r in range(ROWS)
    ]
    for x in range(4)
    for zl in range(8)
]


def window_pairs():
    pairs = []
    for row in range(ROWS):
        for col in range(COLS):
            x, z_lo = col // 8, col % 8
            place = row // 2 % 2 * 4 + col % 2 * 2 + row % 2
            source_row = col // 2
            source_col = (row // 4 + 2) % 4 * 8 + (place - TURN[z_lo // 2]) % 8
            pairs.append((source_row * COLS + source_col, row * COLS + col))
    return pairs


TURN = (0, 7, 1, 0)


def exchange(parts, groups):
    return lax.all_to_all(parts, ("row", "col"), 0, 0, axis_index_groups=groups)


C = 64
I = 128
J = 64
G = 8


def dot(a, b):
    return lax.dot_general(a, b, (((1,), (0,)), ((), ())), preferred_element_type=F32)


def dot_lanes(a, b):
    return lax.dot_general(a, b, (((1,), (1,)), ((), ())), preferred_element_type=F32)


def split_dot(x, picks):
    high = x.astype(BF16)
    low = (x - high.astype(F32)).astype(BF16)
    return dot(high, picks) + dot(low, picks)


def neighbours(value, ends, lane):
    before = jnp.where(lane < 8, ends, pltpu.roll(value, 8, 1)).astype(BF16)
    after = jnp.where(lane >= 120, ends, pltpu.roll(value, I - 8, 1)).astype(BF16)
    return before, value.astype(BF16), after


def back_kernel(cot, w, ga, gae):
    lane = lax.broadcasted_iota(jnp.int32, (C, I), 1)
    slot = lane % 16
    weights = jnp.concatenate(
        [jnp.concatenate([w[3 * a + b] for a in range(3)], axis=1) for b in range(3)], axis=0
    )
    edge_weights = jnp.concatenate(
        [jnp.concatenate([w[b], w[6 + b]], axis=1) for b in range(3)], axis=0
    )

    def put(ref, place, value, fresh):
        ref[place] = value if fresh else ref[place] + value

    def back(k, first):
        fresh = [first, first, True]
        packed = jnp.zeros((C, I), F32)
        for p in range(0, G, 2):
            stacks = []
            for q in (p, p + 1):
                x = cot[G * k + q]
                wide = x.astype(F32)
                later = jnp.where(lane < 120, pltpu.roll(wide, I - 8, 1), 0.0).astype(BF16)
                earlier = jnp.where(lane >= 8, pltpu.roll(wide, 8, 1), 0.0).astype(BF16)
                stacks.append(jnp.concatenate([later, x, earlier], axis=0))
                packed = jnp.where(lane // 16 == q, pltpu.roll(wide, (16 * q + 8) % I, 1), packed)
            part = dot(weights, jnp.concatenate(stacks, axis=1))
            for b in range(3):
                for n, q in enumerate((p, p + 1)):
                    value = part[C * b : C * b + C, I * n : I * n + I]
                    put(ga, G * (k + b) + q, value, fresh[b])
        both = jnp.concatenate(
            [jnp.where(slot >= 8, packed, 0.0), jnp.where(slot < 8, packed, 0.0)], axis=0
        ).astype(BF16)
        part = dot(edge_weights, both)
        for b in range(3):
            put(gae, k + b, part[C * b : C * b + C], fresh[b])

    back(0, True)

    @pl.loop(1, 8)
    def _(k):
        back(k, False)


def fold8(tiles, lane):
    for step in (16, 32, 64):
        low = lane & step == 0
        tiles = [
            jnp.where(low, x, y) + pltpu.roll(jnp.where(low, y, x), step, 1)
            for x, y in zip(tiles[::2], tiles[1::2])
        ]
    return tiles[0]


def main_kernel(cot, ga, gae, own, ends, window, ids, out, act_out, edge_out, gk, acc, half, col_t):
    step = pl.program_id(0)
    lane = lax.broadcasted_iota(jnp.int32, (C, I), 1)
    thin = lax.broadcasted_iota(jnp.int32, (16, I), 1)
    m0 = lax.broadcasted_iota(jnp.int32, (I, I), 0)
    m1 = lax.broadcasted_iota(jnp.int32, (I, I), 1)

    @pl.when(step == 0)
    def _():
        acc[...] = jnp.zeros_like(acc)
        gk[...] = jnp.zeros_like(gk)
        row, col = ids[0], ids[1]
        block = col // 2
        low = ends[jnp.maximum(row - 1, 0)].astype(F32)[G:]
        high = ends[jnp.minimum(row + 1, ROWS - 1)].astype(F32)[:G]
        edge = jnp.concatenate([high, low], axis=0)
        half[:, :I] = own[...].astype(F32).T * 0.5
        half[:, I:] = jnp.concatenate([edge] * 8, axis=0).T * 0.5
        inner = window[...].astype(F32)
        low = ends[jnp.maximum(block - 1, 0)].astype(F32)[G:]
        high = ends[jnp.minimum(block + 1, ROWS - 1)].astype(F32)[:G]
        wide = jnp.where(
            col % 2 == 0, jnp.concatenate([low, inner], axis=0), jnp.concatenate([inner, high], axis=0)
        )
        col_t[...] = jnp.concatenate([wide, jnp.zeros((I - 80, I), F32)], axis=0).T

    def gate(h):
        t = jnp.tanh(h)
        p = 1.0 + t
        y = h * p
        return y, p + y * (1.0 - t)

    def group(k, taps, mask):
        spread = (m0 == G * k + m1 // 16).astype(BF16)
        gather = (m1 == G * k + m0 // 16).astype(BF16)
        wide = col_t[...]
        here = dot(wide.astype(BF16), spread)
        edge_on = jnp.where(
            lane % 16 < 8, (ids[0] < ROWS - 1).astype(F32), (ids[0] > 0).astype(F32)
        )
        if mask is not None:
            edge_on = edge_on * mask
        y, slope = gate(half[:C, I:] * here[:C] + (half[C:, I:] + 0.5 * here[C:]))
        edge_act = y * edge_on
        edge_out[0] = edge_act.astype(BF16)
        g_edge = gae[k] * (slope * edge_on)
        acc[4] += g_edge * here[:C]
        acc[5] += g_edge
        near = pltpu.roll(wide, (I - G * k) % I, 1)
        ends_q = [pltpu.roll(edge_act, (I - 16 * q - 8) % I, 1) for q in range(G)]
        pieces = [[[None] * 4 for _ in range(3)] for _ in range(G)]
        sums = []
        for n in range(4):
            part = slice(16 * n, 16 * n + 16)
            u_half, v_half = half[part, :I], half[C + 16 * n : C + 16 * n + 16, :I]
            row_u = row_v = 0.0
            g_u, g_v = [], []
            for q in range(G):
                uc = near[part, q : q + 1]
                vc = near[C + 16 * n : C + 16 * n + 16, q : q + 1] * 0.5
                y, slope = gate(u_half * uc + (v_half + vc))
                g = ga[q, part] * slope
                if mask is not None:
                    y, g = y * mask, g * mask
                three = neighbours(y, ends_q[q][part], thin)
                for a in range(3):
                    pieces[q][a][n] = three[a]
                act_out[q, part] = three[1]
                row_u += g * uc
                row_v += g
                g_u.append(g * u_half)
                g_v.append(g)
            acc[0, part] += row_u
            acc[1, part] += row_v
            sums.append((fold8(g_u, thin), fold8(g_v, thin)))
        for m, g in ((0, g_edge * half[:C, I:]), (1, g_edge)):
            folded = jnp.concatenate([x[m] for x in sums], axis=0) + g
            acc[2 + m] += split_dot(folded, gather)
        acts = jnp.concatenate(
            [jnp.concatenate([t for a in range(3) for t in pieces[q][a]], axis=0) for q in range(G)],
            axis=1,
        )
        cots = jnp.concatenate(
            [jnp.concatenate([cot[G * (k - b) + q] for q in range(G)], axis=1) for b in taps], axis=0
        )
        gk[:, C * taps[0] : C * (taps[-1] + 1)] += dot_lanes(acts, cots)

    pl.when(step == 0)(lambda: group(0, [0], (ids[1] > 0).astype(F32)))
    pl.when(step == 1)(lambda: group(1, [0, 1], None))
    pl.when((step > 1) & (step < 8))(lambda: group(step, [0, 1, 2], None))
    pl.when(step == 8)(lambda: group(8, [1, 2], None))
    pl.when(step == 9)(lambda: group(9, [2], (ids[1] < COLS - 1).astype(F32)))

    def folded(x):
        x = x + pltpu.roll(x, 64, 1)
        x = x + pltpu.roll(x, 32, 1)
        return x + pltpu.roll(x, 16, 1)

    @pl.when(step == 9)
    def _():
        big_lane = lax.broadcasted_iota(jnp.int32, (2 * C, I), 1)
        outer = pltpu.roll(folded(jnp.concatenate([acc[4], acc[5]], axis=0)), 80, 1) * 0.5
        sums = jnp.concatenate([acc[2], acc[3] * 0.5], axis=0)
        total = gk[...]
        rest = jnp.concatenate([total[: 2 * C, 128:160]] * 4, axis=1)
        misc = jnp.where(big_lane < 80, sums, jnp.where(big_lane < 96, outer, rest))
        tail = jnp.concatenate([total[128:, 128:], total[:64, 160:], total[64:128, 160:]], axis=1)
        rows = jnp.concatenate([acc[0], acc[1]], axis=0) * 0.5
        for t in range(32):
            if t < 24:
                out[t, :8] = total[8 * t : 8 * t + 8, :128]
            else:
                out[t, :8] = tail[8 * (t - 24) : 8 * (t - 24) + 8]
            out[t, 8:12] = rows[4 * t : 4 * t + 4]
            out[t, 12:16] = misc[4 * t : 4 * t + 4]


def whole(shape, dtype):
    return jax.ShapeDtypeStruct(shape, dtype)


VMEM = pl.BlockSpec(memory_space=pltpu.VMEM)
SMEM = pl.BlockSpec(memory_space=pltpu.SMEM)


def run_back(cot, w):
    return pl.pallas_call(
        back_kernel,
        out_shape=(whole((80, C, I), F32), whole((10, C, I), F32)),
        in_specs=[VMEM] * 2,
        out_specs=(VMEM, VMEM),
        compiler_params=pltpu.CompilerParams(vmem_limit_bytes=40 * 2**20),
        cost_estimate=pl.CostEstimate(flops=2_400_000_000, bytes_accessed=4_000_000, transcendentals=0),
        name="tile_back",
    )(cot, w)


def run_main(cot, ga, gae, own, ends, window, ids):
    def group(shape):
        return pl.BlockSpec((shape, C, I), lambda k: (k, 0, 0))

    return pl.pallas_call(
        main_kernel,
        grid=(10,),
        out_shape=(whole((32, 16, I), F32), whole((80, C, I), BF16), whole((10, C, I), BF16)),
        in_specs=[VMEM, group(G), VMEM, VMEM, VMEM, VMEM, SMEM],
        out_specs=(VMEM, group(G), group(1)),
        scratch_shapes=[
            pltpu.VMEM((192, 192), F32),
            pltpu.VMEM((6, C, I), F32),
            pltpu.VMEM((2 * C, 2 * I), F32),
            pltpu.VMEM((2 * C, I), F32),
        ],
        compiler_params=pltpu.CompilerParams(vmem_limit_bytes=40 * 2**20),
        cost_estimate=pl.CostEstimate(flops=1_300_000_000, bytes_accessed=6_000_000, transcendentals=700_000),
        name="tile_gradients",
    )(cot, ga, gae, own, ends, window, ids)


def forward_kernel(act, edge, w, out):
    lane = lax.broadcasted_iota(jnp.int32, (C, I), 1)
    weights = w[...]

    def group(k, taps):
        edge_act = edge[k].astype(F32)
        for p in range(0, G, 2):
            stacks = []
            for q in (p, p + 1):
                ends = pltpu.roll(edge_act, (I - 16 * q - 8) % I, 1)
                stacks.append(jnp.concatenate(neighbours(act[G * k + q].astype(F32), ends, lane), axis=0))
            stack = jnp.concatenate(stacks, axis=1)
            part = dot(weights[C * taps[0] : C * (taps[-1] + 1)], stack)
            for n, b in enumerate(taps):
                for h, q in enumerate((p, p + 1)):
                    value = part[C * n : C * n + C, I * h : I * h + I]
                    place = G * (k - b) + q
                    out[place] = value if b == 0 else out[place] + value

    group(0, [0])
    group(1, [0, 1])

    @pl.loop(2, 8)
    def _(k):
        group(k, [0, 1, 2])

    group(8, [1, 2])
    group(9, [2])


def run_forward(act, edge, w):
    return pl.pallas_call(
        forward_kernel,
        out_shape=whole((J, C, I), F32),
        in_specs=[VMEM] * 3,
        out_specs=VMEM,
        compiler_params=pltpu.CompilerParams(vmem_limit_bytes=40 * 2**20),
        cost_estimate=pl.CostEstimate(flops=700_000_000, bytes_accessed=3_500_000, transcendentals=0),
        name="tile_forward",
    )(act, edge, w)


def reduce_all(parts, z_hi):
    got = exchange(parts, PLANE_GROUPS)
    kernel_sum = jnp.sum(got[:, :8], axis=0)
    rest_sum = jnp.sum(got[:, 12:, 96:], axis=0)
    by_row = got.reshape(8, 4, 16, 128)
    row_main = jnp.sum(by_row[:, :, 8:12], axis=1).reshape(32, 128)
    row_edge = jnp.sum(by_row[:, :, 12:, 80:96], axis=1).reshape(32, 16)
    col_wide = jnp.sum(by_row[:, :, 12:, :80], axis=0).reshape(16, 80)
    tail = jnp.concatenate(
        [col_wide, row_edge[:16], row_edge[16:], rest_sum.reshape(16, 8), jnp.zeros((16, 8), F32)], axis=1
    )
    share = jnp.concatenate([kernel_sum, row_main, tail], axis=0).astype(BF16)
    got = exchange(jnp.broadcast_to(share[None], (16, 56, 128)), LINE_GROUPS).astype(F32)
    kernel_sum = jnp.sum(got[:, :8], axis=0)
    rest_sum = jnp.sum(got[:, 40:, 112:120], axis=0).reshape(4, 32)
    halves = got.reshape(2, 8, 56, 128)
    mine = lax.dynamic_index_in_dim(halves, z_hi, 0, keepdims=False)
    total = jnp.sum(mine[:, 8:40], axis=0).reshape(4, 2, 4, 128)
    edges = jnp.sum(halves[:, :, 40:, 80:112], axis=1)
    edges = jnp.concatenate([edges[:, :, :16], edges[:, :, 16:]], axis=1).reshape(2, 4, 2, 4, 16)
    edges = edges.transpose(1, 0, 2, 3, 4).reshape(16, 4, 16)
    none = jnp.zeros((1, 4, 8), F32)
    from_left = jnp.concatenate([none, edges[:-1, :, :8]], axis=0)
    from_right = jnp.concatenate([edges[1:, :, 8:], none], axis=0)
    cols = jnp.sum(halves[:, :, 40:, :80], axis=0).reshape(8, 4, 4, 80)
    cols = cols.transpose(1, 0, 2, 3).reshape(32, 4, 80)
    low = jnp.concatenate([none, cols[:-1, :, 72:]], axis=0)
    high = jnp.concatenate([cols[1:, :, :8], none], axis=0)
    inner = cols[:, :, 8:72]
    inner = jnp.concatenate([inner[:, :, :8] + low, inner[:, :, 8:56], inner[:, :, 56:] + high], axis=2)
    inner = inner.reshape(16, 2, 4, 64).transpose(0, 2, 1, 3).reshape(16, 4, 128)
    inner = jnp.concatenate(
        [inner[:, :, :8] + from_left, inner[:, :, 8:120], inner[:, :, 120:] + from_right], axis=2
    )
    inner = lax.dynamic_index_in_dim(inner.reshape(4, 2, 2, 4, 128), z_hi, 1, keepdims=False)
    total = (total + inner).reshape(8, 1, 4, 128)
    total = jnp.broadcast_to(total, (8, 4, 4, 128)).reshape(32, 4, 128)
    rest_sum = jnp.pad(rest_sum, ((0, 0), (0, 96)))
    done = jnp.concatenate([kernel_sum, rest_sum], axis=0)
    done = jnp.broadcast_to(done[None], (32, 12, 128))
    got = exchange(jnp.concatenate([done, total], axis=1), PLANE_GROUPS)
    main = got[:, :8].reshape(256, 128)
    rest = got[:, 8:12, :32].reshape(128, 32)
    right = jnp.concatenate([rest, jnp.concatenate([main[192:, 64:96], main[192:, 96:]], axis=0)], axis=1)
    right = jnp.concatenate([right, main[192:, :64]], axis=0)
    gk = jnp.concatenate([main[:192], right], axis=1)
    return gk, got[:, 12:].reshape(128, 128)


def on_device(embedding, kernel, cotangent):
    rows_local = embedding.shape[0]
    bin_count = rows_local * ROWS
    row_id = lax.axis_index("row")
    col_id = lax.axis_index("col")
    place = (col_id % 8 + sum(jnp.where(row_id % 4 == n, turn, 0) for n, turn in enumerate(TURN))) % 8
    mine = lax.dynamic_slice_in_dim(embedding, place // 2 % 2 * (J - G), J + G, 0)
    window = lax.ppermute(mine, ("row", "col"), window_pairs())
    ends = jnp.concatenate([embedding[:G], embedding[rows_local - G :]], axis=0)
    ends = exchange(jnp.broadcast_to(ends[None], (ROWS,) + ends.shape), ROW_GROUPS)
    ids = jnp.stack([row_id, col_id])
    cot = cotangent.transpose(1, 2, 0)
    ga, gae = run_back(cot, kernel.reshape(9, C, C))
    parts, act, edge = run_main(cot, ga, gae, embedding, ends, window, ids)
    taps = kernel.transpose(1, 3, 0, 2).reshape(192, 192)
    prediction = run_forward(act, edge, taps).transpose(2, 0, 1)
    gk, ge = reduce_all(parts, row_id // 2 % 2)
    gk = gk.reshape(3, C, 3, C).transpose(0, 2, 1, 3)
    return prediction, gk / bin_count, ge.T * float(bin_count) ** (-0.5)


def solution(mesh):
    in_specs = (P("row", None), P(), P("row", "col", None))
    out_specs = (P("row", "col", None), P(), P("row", None))
    return jax.shard_map(
        on_device, mesh=mesh, in_specs=in_specs, out_specs=out_specs, check_vma=False
    )
```

```python
import jax
import jax.numpy as jnp
from jax import lax
from jax.experimental import pallas as pl
from jax.experimental.pallas import tpu as pltpu
from jax.sharding import PartitionSpec as P

BF16 = jnp.bfloat16
F32 = jnp.float32

ROWS, COLS = 16, 32


def device_id(y, z_hi, core, x, z_lo):
    return (y * 4 + z_hi * 2 + core) * COLS + x * 8 + z_lo


PLANE_GROUPS = [
    [device_id(y, zh, k, x, zl) for k in range(2) for y in range(4) for x in range(4)]
    for zh in range(2)
    for zl in range(8)
]
LINE_GROUPS = [
    [device_id(y, zh, k, x, zl) for zh in range(2) for zl in range(8)]
    for y in range(4)
    for k in range(2)
    for x in range(4)
]
ROW_GROUPS = [
    [
        device_id(r // 4, r // 2 % 2, r % 2, x, (zl + 4 * (r // 2 % 2)) % 8)
        for r in range(ROWS)
    ]
    for x in range(4)
    for zl in range(8)
]


def window_pairs():
    pairs = []
    for row in range(ROWS):
        for col in range(COLS):
            x, z_lo = col // 8, col % 8
            place = row // 2 % 2 * 4 + col % 2 * 2 + row % 2
            source_row = col // 2
            source_col = (row // 4 + 2) % 4 * 8 + (place - TURN[z_lo // 2]) % 8
            pairs.append((source_row * COLS + source_col, row * COLS + col))
    return pairs


TURN = (0, 7, 1, 0)


def exchange(parts, groups):
    return lax.all_to_all(parts, ("row", "col"), 0, 0, axis_index_groups=groups)


C = 64
I = 128
J = 64
G = 8


def dot(a, b):
    return lax.dot_general(a, b, (((1,), (0,)), ((), ())), preferred_element_type=F32)


def dot_lanes(a, b):
    return lax.dot_general(a, b, (((1,), (1,)), ((), ())), preferred_element_type=F32)


def split_dot(x, picks):
    high = x.astype(BF16)
    low = (x - high.astype(F32)).astype(BF16)
    return dot(high, picks) + dot(low, picks)


def neighbours(value, ends, lane):
    before = jnp.where(lane < 8, ends, pltpu.roll(value, 8, 1))
    after = jnp.where(lane >= 120, ends, pltpu.roll(value, I - 8, 1))
    return before, value, after


def back_kernel(cot, w, ga, gae):
    lane = lax.broadcasted_iota(jnp.int32, (C, I), 1)
    slot = lane % 16
    weights = jnp.concatenate(
        [jnp.concatenate([w[3 * a + b] for a in range(3)], axis=1) for b in range(3)], axis=0
    )
    edge_weights = jnp.concatenate(
        [jnp.concatenate([w[b], w[6 + b]], axis=1) for b in range(3)], axis=0
    )

    def put(ref, place, value, fresh):
        ref[place] = value if fresh else ref[place] + value

    def back(k, first):
        fresh = [first, first, True]
        packed = jnp.zeros((C, I), F32)
        for p in range(0, G, 2):
            stacks = []
            for q in (p, p + 1):
                x = cot[G * k + q]
                wide = x.astype(F32)
                later = jnp.where(lane < 120, pltpu.roll(wide, I - 8, 1), 0.0).astype(BF16)
                earlier = jnp.where(lane >= 8, pltpu.roll(wide, 8, 1), 0.0).astype(BF16)
                stacks.append(jnp.concatenate([later, x, earlier], axis=0))
                packed = jnp.where(lane // 16 == q, pltpu.roll(wide, (16 * q + 8) % I, 1), packed)
            part = dot(weights, jnp.concatenate(stacks, axis=1))
            for b in range(3):
                for n, q in enumerate((p, p + 1)):
                    value = part[C * b : C * b + C, I * n : I * n + I]
                    put(ga, G * (k + b) + q, value, fresh[b])
        both = jnp.concatenate(
            [jnp.where(slot >= 8, packed, 0.0), jnp.where(slot < 8, packed, 0.0)], axis=0
        ).astype(BF16)
        part = dot(edge_weights, both)
        for b in range(3):
            put(gae, k + b, part[C * b : C * b + C], fresh[b])

    back(0, True)

    @pl.loop(1, 8)
    def _(k):
        back(k, False)


def fold8(tiles, lane):
    for step in (16, 32, 64):
        low = lane & step == 0
        tiles = [
            jnp.where(low, x, y) + pltpu.roll(jnp.where(low, y, x), step, 1)
            for x, y in zip(tiles[::2], tiles[1::2])
        ]
    return tiles[0]


def main_kernel(
    cot, ga, gae, own, ends, window, ids, out, act_out, edge_out, gk, acc, half, col_t, expand
):
    lane = lax.broadcasted_iota(jnp.int32, (C, I), 1)
    thin = lax.broadcasted_iota(jnp.int32, (16, I), 1)
    m0 = lax.broadcasted_iota(jnp.int32, (I, I), 0)
    m1 = lax.broadcasted_iota(jnp.int32, (I, I), 1)
    acc[...] = jnp.zeros_like(acc)
    gk[...] = jnp.zeros_like(gk)
    for q in range(G):
        expand[:, I * q : I * q + I] = (m0 == q).astype(BF16)
    row, col = ids[0], ids[1]
    block = col // 2
    low = ends[jnp.maximum(row - 1, 0)].astype(F32)[G:]
    high = ends[jnp.minimum(row + 1, ROWS - 1)].astype(F32)[:G]
    edge = jnp.concatenate([high, low], axis=0)
    half[:, :I] = own[...].astype(F32).T * 0.5
    half[:, I:] = jnp.concatenate([edge] * 8, axis=0).T * 0.5
    inner = window[...].astype(F32)
    low = ends[jnp.maximum(block - 1, 0)].astype(F32)[G:]
    high = ends[jnp.minimum(block + 1, ROWS - 1)].astype(F32)[:G]
    wide = jnp.where(
        col % 2 == 0, jnp.concatenate([low, inner], axis=0), jnp.concatenate([inner, high], axis=0)
    )
    col_t[...] = jnp.concatenate([wide, jnp.zeros((I - 80, I), F32)], axis=0).T

    def gate(h):
        t = jnp.tanh(h)
        p = 1.0 + t
        y = h * p
        return y, p + y * (1.0 - t)

    def group(k, taps, mask):
        spread = (m0 == G * k + m1 // 16).astype(BF16)
        gather = (m1 == G * k + m0 // 16).astype(BF16)
        wide = col_t[...]
        here = dot(wide.astype(BF16), spread)
        edge_on = jnp.where(
            lane % 16 < 8, (ids[0] < ROWS - 1).astype(F32), (ids[0] > 0).astype(F32)
        )
        if mask is not None:
            edge_on = edge_on * mask
        y, slope = gate(half[:C, I:] * here[:C] + (half[C:, I:] + 0.5 * here[C:]))
        edge_act = y * edge_on
        edge_act = edge_act.astype(BF16)
        edge_out[k] = edge_act
        g_edge = gae[k] * (slope * edge_on)
        acc[4] += g_edge * here[:C]
        acc[5] += g_edge
        near = pltpu.roll(wide, (I - G * k) % I, 1)
        near = jnp.concatenate([near[:C], near[C:] * 0.5], axis=0).astype(BF16)
        near = dot(near, expand[...])
        ends_q = [pltpu.roll(edge_act, (I - 16 * q - 8) % I, 1) for q in range(G)]
        pieces = [[[None] * 4 for _ in range(3)] for _ in range(G)]
        sums = []
        for n in range(4):
            part = slice(16 * n, 16 * n + 16)
            u_half, v_half = half[part, :I], half[C + 16 * n : C + 16 * n + 16, :I]
            row_u = row_v = 0.0
            g_u, g_v = [], []
            for q in range(G):
                uc = near[part, I * q : I * q + I]
                vc = near[C + 16 * n : C + 16 * n + 16, I * q : I * q + I]
                y, slope = gate(u_half * uc + (v_half + vc))
                g = ga[G * k + q, part] * slope
                if mask is not None:
                    y, g = y * mask, g * mask
                three = neighbours(y.astype(BF16), ends_q[q][part], thin)
                for a in range(3):
                    pieces[q][a][n] = three[a]
                act_out[G * k + q, part] = three[1]
                row_u += g * uc
                row_v += g
                g_u.append(g * u_half)
                g_v.append(g)
            acc[0, part] += row_u
            acc[1, part] += row_v
            sums.append((fold8(g_u, thin), fold8(g_v, thin)))
        for m, g in ((0, g_edge * half[:C, I:]), (1, g_edge)):
            folded = jnp.concatenate([x[m] for x in sums], axis=0) + g
            acc[2 + m] += split_dot(folded, gather)
        acts = jnp.concatenate(
            [jnp.concatenate([t for a in range(3) for t in pieces[q][a]], axis=0) for q in range(G)],
            axis=1,
        )
        cots = jnp.concatenate(
            [jnp.concatenate([cot[G * (k - b) + q] for q in range(G)], axis=1) for b in taps], axis=0
        )
        gk[:, C * taps[0] : C * (taps[-1] + 1)] += dot_lanes(acts, cots)

    group(0, [0], (col > 0).astype(F32))
    group(1, [0, 1], None)

    @pl.loop(2, 8)
    def _(k):
        group(k, [0, 1, 2], None)

    group(8, [1, 2], None)
    group(9, [2], (col < COLS - 1).astype(F32))

    def folded(x):
        x = x + pltpu.roll(x, 64, 1)
        x = x + pltpu.roll(x, 32, 1)
        return x + pltpu.roll(x, 16, 1)

    big_lane = lax.broadcasted_iota(jnp.int32, (2 * C, I), 1)
    outer = pltpu.roll(folded(jnp.concatenate([acc[4], acc[5]], axis=0)), 80, 1) * 0.5
    sums = jnp.concatenate([acc[2], acc[3] * 0.5], axis=0)
    total = gk[...]
    rest = jnp.concatenate([total[: 2 * C, 128:160]] * 4, axis=1)
    misc = jnp.where(big_lane < 80, sums, jnp.where(big_lane < 96, outer, rest))
    tail = jnp.concatenate([total[128:, 128:], total[:64, 160:], total[64:128, 160:]], axis=1)
    rows = jnp.concatenate([acc[0], acc[1]], axis=0) * 0.5
    for t in range(32):
        if t < 24:
            out[t, :8] = total[8 * t : 8 * t + 8, :128]
        else:
            out[t, :8] = tail[8 * (t - 24) : 8 * (t - 24) + 8]
        out[t, 8:12] = rows[4 * t : 4 * t + 4]
        out[t, 12:16] = misc[4 * t : 4 * t + 4]


def whole(shape, dtype):
    return jax.ShapeDtypeStruct(shape, dtype)


VMEM = pl.BlockSpec(memory_space=pltpu.VMEM)
SMEM = pl.BlockSpec(memory_space=pltpu.SMEM)


def run_back(cot, w):
    return pl.pallas_call(
        back_kernel,
        out_shape=(whole((80, C, I), F32), whole((10, C, I), F32)),
        in_specs=[VMEM, VMEM],
        out_specs=(VMEM, VMEM),
        compiler_params=pltpu.CompilerParams(vmem_limit_bytes=12 * 2**20),
        cost_estimate=pl.CostEstimate(flops=2_400_000_000, bytes_accessed=4_000_000, transcendentals=0),
        name="tile_back",
    )(cot, w)


def run_main(cot, ga, gae, own, ends, window, ids):
    return pl.pallas_call(
        main_kernel,
        out_shape=(whole((32, 16, I), F32), whole((80, C, I), BF16), whole((10, C, I), BF16)),
        in_specs=[VMEM] * 6 + [SMEM],
        out_specs=(VMEM, VMEM, VMEM),
        scratch_shapes=[
            pltpu.VMEM((192, 192), F32),
            pltpu.VMEM((6, C, I), F32),
            pltpu.VMEM((2 * C, 2 * I), F32),
            pltpu.VMEM((2 * C, I), F32),
            pltpu.VMEM((I, G * I), BF16),
        ],
        compiler_params=pltpu.CompilerParams(vmem_limit_bytes=12 * 2**20),
        cost_estimate=pl.CostEstimate(flops=1_300_000_000, bytes_accessed=6_000_000, transcendentals=700_000),
        name="tile_gradients",
    )(cot, ga, gae, own, ends, window, ids)


def forward_kernel(act, edge, w, out):
    lane = lax.broadcasted_iota(jnp.int32, (C, I), 1)
    weights = w[...]

    def group(k, taps):
        edge_act = edge[k]
        for p in range(0, G, 2):
            stacks = []
            for q in (p, p + 1):
                ends = pltpu.roll(edge_act, (I - 16 * q - 8) % I, 1)
                stacks.append(jnp.concatenate(neighbours(act[G * k + q], ends, lane), axis=0))
            stack = jnp.concatenate(stacks, axis=1)
            part = dot(weights[C * taps[0] : C * (taps[-1] + 1)], stack)
            for n, b in enumerate(taps):
                for h, q in enumerate((p, p + 1)):
                    value = part[C * n : C * n + C, I * h : I * h + I]
                    place = G * (k - b) + q
                    out[place] = value if b == 0 else out[place] + value

    group(0, [0])
    group(1, [0, 1])

    @pl.loop(2, 8)
    def _(k):
        group(k, [0, 1, 2])

    group(8, [1, 2])
    group(9, [2])


def run_forward(act, edge, w):
    return pl.pallas_call(
        forward_kernel,
        out_shape=whole((J, C, I), F32),
        in_specs=[VMEM] * 3,
        out_specs=VMEM,
        compiler_params=pltpu.CompilerParams(vmem_limit_bytes=40 * 2**20),
        cost_estimate=pl.CostEstimate(flops=700_000_000, bytes_accessed=3_500_000, transcendentals=0),
        name="tile_forward",
    )(act, edge, w)


def swap_rows(x):
    return pltpu.roll(x, 4, 0)


def share_kernel(got, out):
    lane = lax.broadcasted_iota(jnp.int32, (8, I), 1)
    low = lax.broadcasted_iota(jnp.int32, (8, I), 0) < 4
    by_row = [sum(got[4 * m + x, 8:16] for x in range(4)) for m in range(8)]
    by_col = [sum(got[4 * m + x, 8:16] for m in range(8)) for x in range(4)]
    weights = sum(got[t, :8] for t in range(32))
    rest = sum(by_col)
    tails = []
    for x in range(4):
        tail = jnp.where(lane < 80, by_col[x], by_row[x])
        tail = jnp.where(lane < 96, tail, pltpu.roll(by_row[4 + x], 16, 1))
        tails.append(jnp.where(lane < 112, tail, pltpu.roll(rest, 16, 1) if x == 0 else rest))
    rows = [jnp.where(low, by_row[m], swap_rows(by_row[m + 1])) for m in range(0, 8, 2)]
    rows += [jnp.where(low, swap_rows(tails[x]), tails[x + 1]) for x in (0, 2)]
    share = jnp.concatenate(rows + [weights], axis=0).astype(BF16)
    for z in range(16):
        out[z] = share


def finish_kernel(got, ids, out):
    lane = lax.broadcasted_iota(jnp.int32, (16, I), 1)
    part = lax.broadcasted_iota(jnp.int32, (16, I), 0)
    first, last = lane < 8, lane >= 120
    z_hi = ids[0] // 2 % 2
    parts = [got[z].astype(F32) for z in range(16)]
    weights = sum(p[48:] for p in parts)
    tails = [p[32:48] for p in parts]
    edges = [sum(tails[8 * h : 8 * h + 8]) for h in range(2)]
    cols = [jnp.where(lane < 80, tails[n] + tails[8 + n], 0.0) for n in range(8)]
    body, from_low, from_high = {}, {}, {}
    for h in range(2):
        for core in range(2):
            n = 4 * h + 2 * core
            left = pltpu.roll(cols[n], I - 8, 1)
            right = pltpu.roll(cols[n + 1], 56, 1)
            body[h, core] = jnp.where(last, 0.0, left) + jnp.where(first, 0.0, right)
            from_low[h, core] = jnp.where(first, pltpu.roll(edges[h], 48 - 16 * core, 1) + right, 0.0)
            from_high[h, core] = jnp.where(last, pltpu.roll(edges[h], 32 - 16 * core, 1) + left, 0.0)
    above = jnp.where(part >= 4, pltpu.roll(from_low[1, 1], 4, 0), 0.0)
    below = jnp.where(part < 12, pltpu.roll(from_high[0, 0], 12, 0), 0.0)
    sums = {
        (0, 0): above + from_high[0, 1],
        (0, 1): from_low[0, 0] + from_high[1, 0],
        (1, 0): from_low[0, 1] + from_high[1, 1],
        (1, 1): from_low[1, 0] + below,
    }
    rest = edges[0] + edges[1]
    small = lax.broadcasted_iota(jnp.int32, (8, I), 1)
    low = lax.broadcasted_iota(jnp.int32, (8, I), 0) < 4
    rest = jnp.where(small < 112, pltpu.roll(swap_rows(rest[:8]), I - 16, 1), rest[:8])
    for core in range(2):
        rows = slice(16 * core, 16 * core + 16)
        main = [sum(p[rows] for p in parts[8 * h : 8 * h + 8]) for h in range(2)]
        total = jnp.where(
            z_hi == 0, main[0] + body[0, core] + sums[0, core], main[1] + body[1, core] + sums[1, core]
        )
        for y in range(4):
            tile = total[8 * (y // 2) : 8 * (y // 2) + 8]
            tile = jnp.where(low, tile if y % 2 == 0 else swap_rows(tile), rest)
            message = jnp.concatenate([weights, tile], axis=0).astype(BF16)
            for x in range(4):
                out[16 * core + 4 * y + x] = message


def unpack_kernel(got, gk, ge):
    parts = [got[t].astype(F32) for t in range(32)]
    main = jnp.concatenate([p[:8] for p in parts], axis=0) * (1.0 / (ROWS * I))
    low = lax.broadcasted_iota(jnp.int32, (8, I), 0) < 4
    pairs = list(zip(parts[::2], parts[1::2]))
    rest = jnp.concatenate([jnp.where(low, swap_rows(p[8:]), q[8:]) for p, q in pairs], axis=0)
    sums = jnp.concatenate([jnp.where(low, p[8:], swap_rows(q[8:])) for p, q in pairs], axis=0)
    rest = rest * (1.0 / (ROWS * I))
    ge[...] = sums.T * float(ROWS * I) ** (-0.5)
    tail = main[192:]
    for a in range(3):
        rows = slice(C * a, C * a + C)
        gk[3 * a] = main[rows, :C]
        gk[3 * a + 1] = main[rows, C:]
        if a == 2:
            gk[3 * a + 2] = tail[:, :C]
        else:
            gk[3 * a + 2] = jnp.concatenate([rest[rows, 96:], tail[:, 64 + 32 * a : 96 + 32 * a]], axis=1)


def small_call(kernel, out_shape, ids, name, **options):
    return pl.pallas_call(
        kernel,
        out_shape=out_shape,
        in_specs=[VMEM] + [SMEM] * ids,
        out_specs=jax.tree.map(lambda _: VMEM, out_shape),
        cost_estimate=pl.CostEstimate(flops=1_000_000, bytes_accessed=500_000, transcendentals=0),
        name=name,
        **options,
    )


def reduce_all(parts, ids, **options):
    got = exchange(parts, PLANE_GROUPS)
    share = small_call(share_kernel, whole((16, 56, I), BF16), 0, "plane_sums", **options)(got)
    got = exchange(share, LINE_GROUPS)
    done = small_call(finish_kernel, whole((32, 16, I), BF16), 1, "line_sums", **options)(got, ids)
    got = exchange(done, PLANE_GROUPS)
    shapes = (whole((9, C, C), F32), whole((2 * C, I), F32))
    return small_call(unpack_kernel, shapes, 0, "unpack", **options)(got)


def on_device(embedding, kernel, cotangent):
    rows_local = embedding.shape[0]
    row_id = lax.axis_index("row")
    col_id = lax.axis_index("col")
    place = (col_id % 8 + sum(jnp.where(row_id % 4 == n, turn, 0) for n, turn in enumerate(TURN))) % 8
    mine = lax.dynamic_slice_in_dim(embedding, place // 2 % 2 * (J - G), J + G, 0)
    window = lax.ppermute(mine, ("row", "col"), window_pairs())
    ends = jnp.concatenate([embedding[:G], embedding[rows_local - G :]], axis=0)
    ends = exchange(jnp.broadcast_to(ends[None], (ROWS,) + ends.shape), ROW_GROUPS)
    ids = jnp.stack([row_id, col_id])
    cot = cotangent.transpose(1, 2, 0)
    ga, gae = run_back(cot, kernel.reshape(9, C, C))
    parts, act, edge = run_main(cot, ga, gae, embedding, ends, window, ids)
    taps = kernel.transpose(1, 3, 0, 2).reshape(192, 192)
    prediction = run_forward(act, edge, taps).transpose(2, 0, 1)
    gk, ge = reduce_all(parts, ids)
    return prediction, gk.reshape(kernel.shape), ge


def solution(mesh):
    in_specs = (P("row", None), P(), P("row", "col", None))
    out_specs = (P("row", "col", None), P(), P("row", None))
    return jax.shard_map(
        on_device, mesh=mesh, in_specs=in_specs, out_specs=out_specs, check_vma=False
    )
```

```python
import jax
import jax.numpy as jnp
from jax import lax
from jax.experimental import pallas as pl
from jax.experimental.pallas import tpu as pltpu
from jax.sharding import PartitionSpec as P

BF16 = jnp.bfloat16
F32 = jnp.float32

ROWS, COLS = 16, 32


def device_id(y, z_hi, core, x, z_lo):
    return (y * 4 + z_hi * 2 + core) * COLS + x * 8 + z_lo


PLANE_GROUPS = [
    [device_id(y, zh, k, x, zl) for k in range(2) for y in range(4) for x in range(4)]
    for zh in range(2)
    for zl in range(8)
]
LINE_GROUPS = [
    [device_id(y, zh, k, x, zl) for zh in range(2) for zl in range(8)]
    for y in range(4)
    for k in range(2)
    for x in range(4)
]
ROW_GROUPS = [
    [
        device_id(r // 4, r // 2 % 2, r % 2, x, (zl + 4 * (r // 2 % 2)) % 8)
        for r in range(ROWS)
    ]
    for x in range(4)
    for zl in range(8)
]


def window_pairs():
    pairs = []
    for row in range(ROWS):
        for col in range(COLS):
            x, z_lo = col // 8, col % 8
            place = row // 2 % 2 * 4 + col % 2 * 2 + row % 2
            source_row = col // 2
            source_col = (row // 4 + 2) % 4 * 8 + (place - TURN[z_lo // 2]) % 8
            pairs.append((source_row * COLS + source_col, row * COLS + col))
    return pairs


TURN = (0, 7, 1, 0)


def exchange(parts, groups):
    return lax.all_to_all(parts, ("row", "col"), 0, 0, axis_index_groups=groups)


C = 64
I = 128
J = 64
G = 8


def dot(a, b):
    return lax.dot_general(a, b, (((1,), (0,)), ((), ())), preferred_element_type=F32)


def dot_lanes(a, b):
    return lax.dot_general(a, b, (((1,), (1,)), ((), ())), preferred_element_type=F32)


def split_dot(x, picks):
    high = x.astype(BF16)
    low = (x - high.astype(F32)).astype(BF16)
    return dot(high, picks) + dot(low, picks)


def neighbours(value, ends, lane):
    before = jnp.where(lane < 8, ends, pltpu.roll(value, 8, 1))
    after = jnp.where(lane >= 120, ends, pltpu.roll(value, I - 8, 1))
    return before, value, after


class Stream:
    def __init__(self, source, target, sems, count):
        self.source, self.target, self.sems, self.count = source, target, sems, count

    def copy(self, k):
        size = self.source.shape[0] // self.count
        place = pl.ds(k * size, size)
        return pltpu.make_async_copy(self.source.at[place], self.target.at[place], self.sems.at[k])

    def start(self, k):
        if isinstance(k, int):
            if k < self.count:
                self.copy(k).start()
        else:
            pl.when(k < self.count)(lambda: self.copy(k).start())

    def wait(self, k):
        self.copy(k).wait()


AHEAD = 3


def back_kernel(cot_hbm, w_hbm, ga_hbm, gae, cot, w, ga, cot_sems, w_sem, ga_sems):
    w_copy = pltpu.make_async_copy(w_hbm, w, w_sem)
    w_copy.start()
    come = Stream(cot_hbm, cot, cot_sems, 8)
    leave = Stream(ga, ga_hbm, ga_sems, 10)
    for k in range(AHEAD):
        come.start(k)
    lane = lax.broadcasted_iota(jnp.int32, (C, I), 1)
    slot = lane % 16
    w_copy.wait()
    weights = jnp.concatenate(
        [jnp.concatenate([w[3 * a + b] for a in range(3)], axis=1) for b in range(3)], axis=0
    )
    edge_weights = jnp.concatenate(
        [jnp.concatenate([w[b], w[6 + b]], axis=1) for b in range(3)], axis=0
    )

    def put(ref, place, value, fresh):
        ref[place] = value if fresh else ref[place] + value

    def back(k, first):
        come.wait(k)
        come.start(k + AHEAD)
        fresh = [first, first, True]
        packed = jnp.zeros((C, I), F32)
        for p in range(0, G, 2):
            stacks = []
            for q in (p, p + 1):
                x = cot[G * k + q]
                wide = x.astype(F32)
                later = jnp.where(lane < 120, pltpu.roll(wide, I - 8, 1), 0.0).astype(BF16)
                earlier = jnp.where(lane >= 8, pltpu.roll(wide, 8, 1), 0.0).astype(BF16)
                stacks.append(jnp.concatenate([later, x, earlier], axis=0))
                packed = jnp.where(lane // 16 == q, pltpu.roll(wide, (16 * q + 8) % I, 1), packed)
            part = dot(weights, jnp.concatenate(stacks, axis=1))
            for b in range(3):
                for n, q in enumerate((p, p + 1)):
                    value = part[C * b : C * b + C, I * n : I * n + I]
                    put(ga, G * (k + b) + q, value, fresh[b])
        both = jnp.concatenate(
            [jnp.where(slot >= 8, packed, 0.0), jnp.where(slot < 8, packed, 0.0)], axis=0
        ).astype(BF16)
        part = dot(edge_weights, both)
        for b in range(3):
            put(gae, k + b, part[C * b : C * b + C], fresh[b])
        leave.start(k)

    back(0, True)

    @pl.loop(1, 8)
    def _(k):
        back(k, False)

    leave.start(8)
    leave.start(9)
    for k in range(10):
        leave.wait(k)


def fold8(tiles, lane):
    for step in (16, 32, 64):
        low = lane & step == 0
        tiles = [
            jnp.where(low, x, y) + pltpu.roll(jnp.where(low, y, x), step, 1)
            for x, y in zip(tiles[::2], tiles[1::2])
        ]
    return tiles[0]


def main_kernel(
    cot, ga_hbm, gae, own, ends, window, ids, out, act_out, edge_out,
    gk, acc, half, col_t, expand, ga, ga_sems,
):
    lane = lax.broadcasted_iota(jnp.int32, (C, I), 1)
    thin = lax.broadcasted_iota(jnp.int32, (16, I), 1)
    m0 = lax.broadcasted_iota(jnp.int32, (I, I), 0)
    m1 = lax.broadcasted_iota(jnp.int32, (I, I), 1)
    come = Stream(ga_hbm, ga, ga_sems, 10)
    for k in range(AHEAD):
        come.start(k)
    acc[...] = jnp.zeros_like(acc)
    gk[...] = jnp.zeros_like(gk)
    for q in range(G):
        expand[:, I * q : I * q + I] = (m0 == q).astype(BF16)
    row, col = ids[0], ids[1]
    block = col // 2
    low = ends[jnp.maximum(row - 1, 0)].astype(F32)[G:]
    high = ends[jnp.minimum(row + 1, ROWS - 1)].astype(F32)[:G]
    edge = jnp.concatenate([high, low], axis=0)
    half[:, :I] = own[...].astype(F32).T * 0.5
    half[:, I:] = jnp.concatenate([edge] * 8, axis=0).T * 0.5
    inner = window[...].astype(F32)
    low = ends[jnp.maximum(block - 1, 0)].astype(F32)[G:]
    high = ends[jnp.minimum(block + 1, ROWS - 1)].astype(F32)[:G]
    wide = jnp.where(
        col % 2 == 0, jnp.concatenate([low, inner], axis=0), jnp.concatenate([inner, high], axis=0)
    )
    col_t[...] = jnp.concatenate([wide, jnp.zeros((I - 80, I), F32)], axis=0).T

    def gate(h):
        t = jnp.tanh(h)
        p = 1.0 + t
        y = h * p
        return y, p + y * (1.0 - t)

    def group(k, taps, mask):
        come.wait(k)
        come.start(k + AHEAD)
        spread = (m0 == G * k + m1 // 16).astype(BF16)
        gather = (m1 == G * k + m0 // 16).astype(BF16)
        wide = col_t[...]
        here = dot(wide.astype(BF16), spread)
        edge_on = jnp.where(
            lane % 16 < 8, (ids[0] < ROWS - 1).astype(F32), (ids[0] > 0).astype(F32)
        )
        if mask is not None:
            edge_on = edge_on * mask
        y, slope = gate(half[:C, I:] * here[:C] + (half[C:, I:] + 0.5 * here[C:]))
        edge_act = y * edge_on
        edge_act = edge_act.astype(BF16)
        edge_out[k] = edge_act
        g_edge = gae[k] * (slope * edge_on)
        acc[4] += g_edge * here[:C]
        acc[5] += g_edge
        near = pltpu.roll(wide, (I - G * k) % I, 1)
        near = jnp.concatenate([near[:C], near[C:] * 0.5], axis=0).astype(BF16)
        near = dot(near, expand[...])
        ends_q = [pltpu.roll(edge_act, (I - 16 * q - 8) % I, 1) for q in range(G)]
        pieces = [[[None] * 4 for _ in range(3)] for _ in range(G)]
        sums = []
        for n in range(4):
            part = slice(16 * n, 16 * n + 16)
            u_half, v_half = half[part, :I], half[C + 16 * n : C + 16 * n + 16, :I]
            row_u = row_v = 0.0
            g_u, g_v = [], []
            for q in range(G):
                uc = near[part, I * q : I * q + I]
                vc = near[C + 16 * n : C + 16 * n + 16, I * q : I * q + I]
                y, slope = gate(u_half * uc + (v_half + vc))
                g = ga[G * k + q, part] * slope
                if mask is not None:
                    y, g = y * mask, g * mask
                three = neighbours(y.astype(BF16), ends_q[q][part], thin)
                for a in range(3):
                    pieces[q][a][n] = three[a]
                act_out[G * k + q, part] = three[1]
                row_u += g * uc
                row_v += g
                g_u.append(g * u_half)
                g_v.append(g)
            acc[0, part] += row_u
            acc[1, part] += row_v
            sums.append((fold8(g_u, thin), fold8(g_v, thin)))
        for m, g in ((0, g_edge * half[:C, I:]), (1, g_edge)):
            folded = jnp.concatenate([x[m] for x in sums], axis=0) + g
            acc[2 + m] += split_dot(folded, gather)
        acts = jnp.concatenate(
            [jnp.concatenate([t for a in range(3) for t in pieces[q][a]], axis=0) for q in range(G)],
            axis=1,
        )
        cots = jnp.concatenate(
            [jnp.concatenate([cot[G * (k - b) + q] for q in range(G)], axis=1) for b in taps], axis=0
        )
        gk[:, C * taps[0] : C * (taps[-1] + 1)] += dot_lanes(acts, cots)

    group(0, [0], (col > 0).astype(F32))
    group(1, [0, 1], None)

    @pl.loop(2, 8)
    def _(k):
        group(k, [0, 1, 2], None)

    group(8, [1, 2], None)
    group(9, [2], (col < COLS - 1).astype(F32))

    def folded(x):
        x = x + pltpu.roll(x, 64, 1)
        x = x + pltpu.roll(x, 32, 1)
        return x + pltpu.roll(x, 16, 1)

    big_lane = lax.broadcasted_iota(jnp.int32, (2 * C, I), 1)
    outer = pltpu.roll(folded(jnp.concatenate([acc[4], acc[5]], axis=0)), 80, 1) * 0.5
    sums = jnp.concatenate([acc[2], acc[3] * 0.5], axis=0)
    total = gk[...]
    rest = jnp.concatenate([total[: 2 * C, 128:160]] * 4, axis=1)
    misc = jnp.where(big_lane < 80, sums, jnp.where(big_lane < 96, outer, rest))
    tail = jnp.concatenate([total[128:, 128:], total[:64, 160:], total[64:128, 160:]], axis=1)
    rows = jnp.concatenate([acc[0], acc[1]], axis=0) * 0.5
    for t in range(32):
        if t < 24:
            out[t, :8] = total[8 * t : 8 * t + 8, :128]
        else:
            out[t, :8] = tail[8 * (t - 24) : 8 * (t - 24) + 8]
        out[t, 8:12] = rows[4 * t : 4 * t + 4]
        out[t, 12:16] = misc[4 * t : 4 * t + 4]


def whole(shape, dtype):
    return jax.ShapeDtypeStruct(shape, dtype)


VMEM = pl.BlockSpec(memory_space=pltpu.VMEM)
HBM = pl.BlockSpec(memory_space=pltpu.HBM)
SMEM = pl.BlockSpec(memory_space=pltpu.SMEM)


def run_back(cot, w):
    return pl.pallas_call(
        back_kernel,
        out_shape=(whole((80, C, I), F32), whole((10, C, I), F32)),
        in_specs=[HBM, HBM],
        out_specs=(HBM, VMEM),
        scratch_shapes=[
            pltpu.VMEM((J, C, I), BF16),
            pltpu.VMEM((9, C, C), BF16),
            pltpu.VMEM((80, C, I), F32),
            pltpu.SemaphoreType.DMA((8,)),
            pltpu.SemaphoreType.DMA,
            pltpu.SemaphoreType.DMA((10,)),
        ],
        compiler_params=pltpu.CompilerParams(vmem_limit_bytes=16 * 2**20),
        cost_estimate=pl.CostEstimate(flops=2_400_000_000, bytes_accessed=4_000_000, transcendentals=0),
        name="tile_back",
    )(cot, w)


def run_main(cot, ga, gae, own, ends, window, ids):
    return pl.pallas_call(
        main_kernel,
        out_shape=(whole((32, 16, I), F32), whole((80, C, I), BF16), whole((10, C, I), BF16)),
        in_specs=[VMEM, HBM] + [VMEM] * 4 + [SMEM],
        out_specs=(VMEM, VMEM, VMEM),
        scratch_shapes=[
            pltpu.VMEM((192, 192), F32),
            pltpu.VMEM((6, C, I), F32),
            pltpu.VMEM((2 * C, 2 * I), F32),
            pltpu.VMEM((2 * C, I), F32),
            pltpu.VMEM((I, G * I), BF16),
            pltpu.VMEM((80, C, I), F32),
            pltpu.SemaphoreType.DMA((10,)),
        ],
        compiler_params=pltpu.CompilerParams(vmem_limit_bytes=16 * 2**20),
        cost_estimate=pl.CostEstimate(flops=1_300_000_000, bytes_accessed=6_000_000, transcendentals=700_000),
        name="tile_gradients",
    )(cot, ga, gae, own, ends, window, ids)


def forward_kernel(act, edge, w, out):
    lane = lax.broadcasted_iota(jnp.int32, (C, I), 1)
    weights = w[...]

    def group(k, taps):
        edge_act = edge[k]
        for p in range(0, G, 2):
            stacks = []
            for q in (p, p + 1):
                ends = pltpu.roll(edge_act, (I - 16 * q - 8) % I, 1)
                stacks.append(jnp.concatenate(neighbours(act[G * k + q], ends, lane), axis=0))
            stack = jnp.concatenate(stacks, axis=1)
            part = dot(weights[C * taps[0] : C * (taps[-1] + 1)], stack)
            for n, b in enumerate(taps):
                for h, q in enumerate((p, p + 1)):
                    value = part[C * n : C * n + C, I * h : I * h + I]
                    place = G * (k - b) + q
                    out[place] = value if b == 0 else out[place] + value

    group(0, [0])
    group(1, [0, 1])

    @pl.loop(2, 8)
    def _(k):
        group(k, [0, 1, 2])

    group(8, [1, 2])
    group(9, [2])


def run_forward(act, edge, w):
    return pl.pallas_call(
        forward_kernel,
        out_shape=whole((J, C, I), F32),
        in_specs=[VMEM] * 3,
        out_specs=VMEM,
        compiler_params=pltpu.CompilerParams(vmem_limit_bytes=16 * 2**20),
        cost_estimate=pl.CostEstimate(flops=700_000_000, bytes_accessed=3_500_000, transcendentals=0),
        name="tile_forward",
    )(act, edge, w)


def cut_kernel(own, ids, window, ends):
    turn = sum(jnp.where(ids[0] % 4 == n, turn, 0) for n, turn in enumerate(TURN))
    odd = (ids[1] + turn) % 8 // 2 % 2
    wide = own[...].astype(F32)
    window[...] = jnp.where(odd == 1, wide[J - G :], wide[: J + G]).astype(BF16)
    both = jnp.concatenate([wide[:G], wide[I - G :]], axis=0).astype(BF16)
    for n in range(ROWS):
        ends[n] = both


def swap_rows(x):
    return pltpu.roll(x, 4, 0)


def share_kernel(got, out):
    lane = lax.broadcasted_iota(jnp.int32, (8, I), 1)
    low = lax.broadcasted_iota(jnp.int32, (8, I), 0) < 4
    by_row = [sum(got[4 * m + x, 8:16] for x in range(4)) for m in range(8)]
    by_col = [sum(got[4 * m + x, 8:16] for m in range(8)) for x in range(4)]
    weights = sum(got[t, :8] for t in range(32))
    rest = sum(by_col)
    tails = []
    for x in range(4):
        tail = jnp.where(lane < 80, by_col[x], by_row[x])
        tail = jnp.where(lane < 96, tail, pltpu.roll(by_row[4 + x], 16, 1))
        tails.append(jnp.where(lane < 112, tail, pltpu.roll(rest, 16, 1) if x == 0 else rest))
    rows = [jnp.where(low, by_row[m], swap_rows(by_row[m + 1])) for m in range(0, 8, 2)]
    rows += [jnp.where(low, swap_rows(tails[x]), tails[x + 1]) for x in (0, 2)]
    share = jnp.concatenate(rows + [weights], axis=0).astype(BF16)
    for z in range(16):
        out[z] = share


def finish_kernel(got, ids, out):
    lane = lax.broadcasted_iota(jnp.int32, (16, I), 1)
    part = lax.broadcasted_iota(jnp.int32, (16, I), 0)
    first, last = lane < 8, lane >= 120
    z_hi = ids[0] // 2 % 2
    parts = [got[z].astype(F32) for z in range(16)]
    weights = sum(p[48:] for p in parts)
    tails = [p[32:48] for p in parts]
    edges = [sum(tails[8 * h : 8 * h + 8]) for h in range(2)]
    cols = [jnp.where(lane < 80, tails[n] + tails[8 + n], 0.0) for n in range(8)]
    body, from_low, from_high = {}, {}, {}
    for h in range(2):
        for core in range(2):
            n = 4 * h + 2 * core
            left = pltpu.roll(cols[n], I - 8, 1)
            right = pltpu.roll(cols[n + 1], 56, 1)
            body[h, core] = jnp.where(last, 0.0, left) + jnp.where(first, 0.0, right)
            from_low[h, core] = jnp.where(first, pltpu.roll(edges[h], 48 - 16 * core, 1) + right, 0.0)
            from_high[h, core] = jnp.where(last, pltpu.roll(edges[h], 32 - 16 * core, 1) + left, 0.0)
    above = jnp.where(part >= 4, pltpu.roll(from_low[1, 1], 4, 0), 0.0)
    below = jnp.where(part < 12, pltpu.roll(from_high[0, 0], 12, 0), 0.0)
    sums = {
        (0, 0): above + from_high[0, 1],
        (0, 1): from_low[0, 0] + from_high[1, 0],
        (1, 0): from_low[0, 1] + from_high[1, 1],
        (1, 1): from_low[1, 0] + below,
    }
    rest = edges[0] + edges[1]
    small = lax.broadcasted_iota(jnp.int32, (8, I), 1)
    low = lax.broadcasted_iota(jnp.int32, (8, I), 0) < 4
    rest = jnp.where(small < 112, pltpu.roll(swap_rows(rest[:8]), I - 16, 1), rest[:8])
    for core in range(2):
        rows = slice(16 * core, 16 * core + 16)
        main = [sum(p[rows] for p in parts[8 * h : 8 * h + 8]) for h in range(2)]
        total = jnp.where(
            z_hi == 0, main[0] + body[0, core] + sums[0, core], main[1] + body[1, core] + sums[1, core]
        )
        for y in range(4):
            tile = total[8 * (y // 2) : 8 * (y // 2) + 8]
            tile = jnp.where(low, tile if y % 2 == 0 else swap_rows(tile), rest)
            message = jnp.concatenate([weights, tile], axis=0).astype(BF16)
            for x in range(4):
                out[16 * core + 4 * y + x] = message


def unpack_kernel(got, gk, ge):
    parts = [got[t].astype(F32) for t in range(32)]
    main = jnp.concatenate([p[:8] for p in parts], axis=0) * (1.0 / (ROWS * I))
    low = lax.broadcasted_iota(jnp.int32, (8, I), 0) < 4
    pairs = list(zip(parts[::2], parts[1::2]))
    rest = jnp.concatenate([jnp.where(low, swap_rows(p[8:]), q[8:]) for p, q in pairs], axis=0)
    sums = jnp.concatenate([jnp.where(low, p[8:], swap_rows(q[8:])) for p, q in pairs], axis=0)
    rest = rest * (1.0 / (ROWS * I))
    ge[...] = sums.T * float(ROWS * I) ** (-0.5)
    tail = main[192:]
    for a in range(3):
        rows = slice(C * a, C * a + C)
        gk[3 * a] = main[rows, :C]
        gk[3 * a + 1] = main[rows, C:]
        if a == 2:
            gk[3 * a + 2] = tail[:, :C]
        else:
            gk[3 * a + 2] = jnp.concatenate([rest[rows, 96:], tail[:, 64 + 32 * a : 96 + 32 * a]], axis=1)


def small_call(kernel, out_shape, ids, name, **options):
    return pl.pallas_call(
        kernel,
        out_shape=out_shape,
        in_specs=[VMEM] + [SMEM] * ids,
        out_specs=jax.tree.map(lambda _: VMEM, out_shape),
        compiler_params=pltpu.CompilerParams(vmem_limit_bytes=6 * 2**20),
        cost_estimate=pl.CostEstimate(flops=1_000_000, bytes_accessed=500_000, transcendentals=0),
        name=name,
        **options,
    )


def reduce_all(parts, ids, **options):
    got = exchange(parts, PLANE_GROUPS)
    share = small_call(share_kernel, whole((16, 56, I), BF16), 0, "plane_sums", **options)(got)
    got = exchange(share, LINE_GROUPS)
    done = small_call(finish_kernel, whole((32, 16, I), BF16), 1, "line_sums", **options)(got, ids)
    got = exchange(done, PLANE_GROUPS)
    shapes = (whole((9, C, C), F32), whole((2 * C, I), F32))
    return small_call(unpack_kernel, shapes, 0, "unpack", **options)(got)


def on_device(embedding, kernel, cotangent):
    row_id = lax.axis_index("row")
    col_id = lax.axis_index("col")
    ids = jnp.stack([row_id, col_id])
    shapes = (whole((J + G, 2 * C), BF16), whole((ROWS, 2 * G, 2 * C), BF16))
    mine, ends = small_call(cut_kernel, shapes, 1, "cut_embedding")(embedding, ids)
    window = lax.ppermute(mine, ("row", "col"), window_pairs())
    ends = exchange(ends, ROW_GROUPS)
    cot = cotangent.transpose(1, 2, 0)
    ga, gae = run_back(cot, kernel.reshape(9, C, C))
    parts, act, edge = run_main(cot, ga, gae, embedding, ends, window, ids)
    taps = kernel.transpose(1, 3, 0, 2).reshape(192, 192)
    prediction = run_forward(act, edge, taps).transpose(2, 0, 1)
    gk, ge = reduce_all(parts, ids)
    return prediction, gk.reshape(kernel.shape), ge


def solution(mesh):
    in_specs = (P("row", None), P(), P("row", "col", None))
    out_specs = (P("row", "col", None), P(), P("row", None))
    return jax.shard_map(
        on_device, mesh=mesh, in_specs=in_specs, out_specs=out_specs, check_vma=False
    )
```

```python
import jax
import jax.numpy as jnp
from jax import lax
from jax.experimental import pallas as pl
from jax.experimental.pallas import tpu as pltpu
from jax.sharding import PartitionSpec as P

BF16 = jnp.bfloat16
F32 = jnp.float32

ROWS, COLS = 16, 32


def device_id(y, z_hi, core, x, z_lo):
    return (y * 4 + z_hi * 2 + core) * COLS + x * 8 + z_lo


PLANE_GROUPS = [
    [device_id(y, zh, k, x, zl) for k in range(2) for y in range(4) for x in range(4)]
    for zh in range(2)
    for zl in range(8)
]
LINE_GROUPS = [
    [device_id(y, zh, k, x, zl) for zh in range(2) for zl in range(8)]
    for y in range(4)
    for k in range(2)
    for x in range(4)
]
ROW_GROUPS = [
    [
        device_id(r // 4, r // 2 % 2, r % 2, x, (zl + 4 * (r // 2 % 2)) % 8)
        for r in range(ROWS)
    ]
    for x in range(4)
    for zl in range(8)
]


def window_pairs():
    pairs = []
    for row in range(ROWS):
        for col in range(COLS):
            x, z_lo = col // 8, col % 8
            place = row // 2 % 2 * 4 + col % 2 * 2 + row % 2
            source_row = col // 2
            source_col = (row // 4 + 2) % 4 * 8 + (place - TURN[z_lo // 2]) % 8
            pairs.append((source_row * COLS + source_col, row * COLS + col))
    return pairs


TURN = (0, 7, 1, 0)


def exchange(parts, groups):
    return lax.all_to_all(parts, ("row", "col"), 0, 0, axis_index_groups=groups)


C = 64
I = 128
J = 64
G = 8


def dot(a, b):
    return lax.dot_general(a, b, (((1,), (0,)), ((), ())), preferred_element_type=F32)


def dot_lanes(a, b):
    return lax.dot_general(a, b, (((1,), (1,)), ((), ())), preferred_element_type=F32)


def split_dot(x, picks):
    high = x.astype(BF16)
    low = (x - high.astype(F32)).astype(BF16)
    return dot(high, picks) + dot(low, picks)


def neighbours(value, ends, lane):
    before = jnp.where(lane < 8, ends, pltpu.roll(value, 8, 1))
    after = jnp.where(lane >= 120, ends, pltpu.roll(value, I - 8, 1))
    return before, value, after


def back(cot, w, ga, gae):
    lane = lax.broadcasted_iota(jnp.int32, (C, I), 1)
    slot = lane % 16
    weights = jnp.concatenate(
        [jnp.concatenate([w[3 * a + b] for a in range(3)], axis=1) for b in range(3)], axis=0
    )
    edge_weights = jnp.concatenate(
        [jnp.concatenate([w[b], w[6 + b]], axis=1) for b in range(3)], axis=0
    )

    def put(ref, place, value, fresh):
        ref[place] = value if fresh else ref[place] + value

    def group(k, first):
        fresh = [first, first, True]
        packed = jnp.zeros((C, I), F32)
        for p in range(0, G, 2):
            stacks = []
            for q in (p, p + 1):
                x = cot[G * k + q]
                wide = x.astype(F32)
                later = jnp.where(lane < 120, pltpu.roll(wide, I - 8, 1), 0.0).astype(BF16)
                earlier = jnp.where(lane >= 8, pltpu.roll(wide, 8, 1), 0.0).astype(BF16)
                stacks.append(jnp.concatenate([later, x, earlier], axis=0))
                packed = jnp.where(lane // 16 == q, pltpu.roll(wide, (16 * q + 8) % I, 1), packed)
            part = dot(weights, jnp.concatenate(stacks, axis=1))
            for b in range(3):
                for n, q in enumerate((p, p + 1)):
                    value = part[C * b : C * b + C, I * n : I * n + I]
                    put(ga, G * (k + b) + q, value, fresh[b])
        both = jnp.concatenate(
            [jnp.where(slot >= 8, packed, 0.0), jnp.where(slot < 8, packed, 0.0)], axis=0
        ).astype(BF16)
        part = dot(edge_weights, both)
        for b in range(3):
            put(gae, k + b, part[C * b : C * b + C], fresh[b])

    group(0, True)

    @pl.loop(1, 8)
    def _(k):
        group(k, False)


def fold8(tiles, lane):
    for step in (16, 32, 64):
        low = lane & step == 0
        tiles = [
            jnp.where(low, x, y) + pltpu.roll(jnp.where(low, y, x), step, 1)
            for x, y in zip(tiles[::2], tiles[1::2])
        ]
    return tiles[0]


def main_kernel(
    cot, w, own, ends, window, ids, out, act_out, edge_out, gk, acc, half, col_t, expand, ga, gae
):
    lane = lax.broadcasted_iota(jnp.int32, (C, I), 1)
    thin = lax.broadcasted_iota(jnp.int32, (16, I), 1)
    m0 = lax.broadcasted_iota(jnp.int32, (I, I), 0)
    m1 = lax.broadcasted_iota(jnp.int32, (I, I), 1)
    back(cot, w, ga, gae)
    acc[...] = jnp.zeros_like(acc)
    gk[...] = jnp.zeros_like(gk)
    for q in range(G):
        expand[:, I * q : I * q + I] = (m0 == q).astype(BF16)
    row, col = ids[0], ids[1]
    block = col // 2
    low = ends[jnp.maximum(row - 1, 0)].astype(F32)[G:]
    high = ends[jnp.minimum(row + 1, ROWS - 1)].astype(F32)[:G]
    edge = jnp.concatenate([high, low], axis=0)
    half[:, :I] = own[...].astype(F32).T * 0.5
    half[:, I:] = jnp.concatenate([edge] * 8, axis=0).T * 0.5
    inner = window[...].astype(F32)
    low = ends[jnp.maximum(block - 1, 0)].astype(F32)[G:]
    high = ends[jnp.minimum(block + 1, ROWS - 1)].astype(F32)[:G]
    wide = jnp.where(
        col % 2 == 0, jnp.concatenate([low, inner], axis=0), jnp.concatenate([inner, high], axis=0)
    )
    col_t[...] = jnp.concatenate([wide, jnp.zeros((I - 80, I), F32)], axis=0).T

    def gate(h):
        t = jnp.tanh(h)
        p = 1.0 + t
        y = h * p
        return y, p + y * (1.0 - t)

    def group(k, taps, mask):
        spread = (m0 == G * k + m1 // 16).astype(BF16)
        gather = (m1 == G * k + m0 // 16).astype(BF16)
        wide = col_t[...]
        here = dot(wide.astype(BF16), spread)
        edge_on = jnp.where(
            lane % 16 < 8, (ids[0] < ROWS - 1).astype(F32), (ids[0] > 0).astype(F32)
        )
        if mask is not None:
            edge_on = edge_on * mask
        y, slope = gate(half[:C, I:] * here[:C] + (half[C:, I:] + 0.5 * here[C:]))
        edge_act = y * edge_on
        edge_act = edge_act.astype(BF16)
        edge_out[k] = edge_act
        g_edge = gae[k] * (slope * edge_on)
        acc[4] += g_edge * here[:C]
        acc[5] += g_edge
        near = pltpu.roll(wide, (I - G * k) % I, 1)
        near = jnp.concatenate([near[:C], near[C:] * 0.5], axis=0).astype(BF16)
        near = dot(near, expand[...])
        ends_q = [pltpu.roll(edge_act, (I - 16 * q - 8) % I, 1) for q in range(G)]
        pieces = [[[None] * 4 for _ in range(3)] for _ in range(G)]
        sums = []
        for n in range(4):
            part = slice(16 * n, 16 * n + 16)
            u_half, v_half = half[part, :I], half[C + 16 * n : C + 16 * n + 16, :I]
            row_u = row_v = 0.0
            g_u, g_v = [], []
            for q in range(G):
                uc = near[part, I * q : I * q + I]
                vc = near[C + 16 * n : C + 16 * n + 16, I * q : I * q + I]
                y, slope = gate(u_half * uc + (v_half + vc))
                g = ga[G * k + q, part] * slope
                if mask is not None:
                    y, g = y * mask, g * mask
                three = neighbours(y.astype(BF16), ends_q[q][part], thin)
                for a in range(3):
                    pieces[q][a][n] = three[a]
                act_out[G * k + q, part] = three[1]
                row_u += g * uc
                row_v += g
                g_u.append(g * u_half)
                g_v.append(g)
            acc[0, part] += row_u
            acc[1, part] += row_v
            sums.append((fold8(g_u, thin), fold8(g_v, thin)))
        for m, g in ((0, g_edge * half[:C, I:]), (1, g_edge)):
            folded = jnp.concatenate([x[m] for x in sums], axis=0) + g
            acc[2 + m] += split_dot(folded, gather)
        acts = jnp.concatenate(
            [jnp.concatenate([t for a in range(3) for t in pieces[q][a]], axis=0) for q in range(G)],
            axis=1,
        )
        cots = jnp.concatenate(
            [jnp.concatenate([cot[G * (k - b) + q] for q in range(G)], axis=1) for b in taps], axis=0
        )
        gk[:, C * taps[0] : C * (taps[-1] + 1)] += dot_lanes(acts, cots)

    group(0, [0], (col > 0).astype(F32))
    group(1, [0, 1], None)

    @pl.loop(2, 8)
    def _(k):
        group(k, [0, 1, 2], None)

    group(8, [1, 2], None)
    group(9, [2], (col < COLS - 1).astype(F32))

    def folded(x):
        x = x + pltpu.roll(x, 64, 1)
        x = x + pltpu.roll(x, 32, 1)
        return x + pltpu.roll(x, 16, 1)

    big_lane = lax.broadcasted_iota(jnp.int32, (2 * C, I), 1)
    outer = pltpu.roll(folded(jnp.concatenate([acc[4], acc[5]], axis=0)), 80, 1) * 0.5
    sums = jnp.concatenate([acc[2], acc[3] * 0.5], axis=0)
    total = gk[...]
    rest = jnp.concatenate([total[: 2 * C, 128:160]] * 4, axis=1)
    misc = jnp.where(big_lane < 80, sums, jnp.where(big_lane < 96, outer, rest))
    tail = jnp.concatenate([total[128:, 128:], total[:64, 160:], total[64:128, 160:]], axis=1)
    rows = jnp.concatenate([acc[0], acc[1]], axis=0) * 0.5
    for t in range(32):
        if t < 24:
            out[t, :8] = total[8 * t : 8 * t + 8, :128]
        else:
            out[t, :8] = tail[8 * (t - 24) : 8 * (t - 24) + 8]
        out[t, 8:12] = rows[4 * t : 4 * t + 4]
        out[t, 12:16] = misc[4 * t : 4 * t + 4]


def whole(shape, dtype):
    return jax.ShapeDtypeStruct(shape, dtype)


VMEM = pl.BlockSpec(memory_space=pltpu.VMEM)
SMEM = pl.BlockSpec(memory_space=pltpu.SMEM)


def run_main(cot, w, own, ends, window, ids):
    return pl.pallas_call(
        main_kernel,
        out_shape=(whole((32, 16, I), F32), whole((80, C, I), BF16), whole((10, C, I), BF16)),
        in_specs=[VMEM] * 5 + [SMEM],
        out_specs=(VMEM, VMEM, VMEM),
        scratch_shapes=[
            pltpu.VMEM((192, 192), F32),
            pltpu.VMEM((6, C, I), F32),
            pltpu.VMEM((2 * C, 2 * I), F32),
            pltpu.VMEM((2 * C, I), F32),
            pltpu.VMEM((I, G * I), BF16),
            pltpu.VMEM((80, C, I), F32),
            pltpu.VMEM((10, C, I), F32),
        ],
        compiler_params=pltpu.CompilerParams(vmem_limit_bytes=12 * 2**20),
        cost_estimate=pl.CostEstimate(flops=3_700_000_000, bytes_accessed=4_000_000, transcendentals=700_000),
        name="tile_gradients",
    )(cot, w, own, ends, window, ids)


def forward_kernel(act, edge, w, out):
    lane = lax.broadcasted_iota(jnp.int32, (C, I), 1)
    weights = w[...]

    def group(k, taps):
        edge_act = edge[k]
        for p in range(0, G, 2):
            stacks = []
            for q in (p, p + 1):
                ends = pltpu.roll(edge_act, (I - 16 * q - 8) % I, 1)
                stacks.append(jnp.concatenate(neighbours(act[G * k + q], ends, lane), axis=0))
            stack = jnp.concatenate(stacks, axis=1)
            part = dot(weights[C * taps[0] : C * (taps[-1] + 1)], stack)
            for n, b in enumerate(taps):
                for h, q in enumerate((p, p + 1)):
                    value = part[C * n : C * n + C, I * h : I * h + I]
                    place = G * (k - b) + q
                    out[place] = value if b == 0 else out[place] + value

    group(0, [0])
    group(1, [0, 1])

    @pl.loop(2, 8)
    def _(k):
        group(k, [0, 1, 2])

    group(8, [1, 2])
    group(9, [2])


def run_forward(act, edge, w):
    return pl.pallas_call(
        forward_kernel,
        out_shape=whole((J, C, I), F32),
        in_specs=[VMEM] * 3,
        out_specs=VMEM,
        compiler_params=pltpu.CompilerParams(vmem_limit_bytes=12 * 2**20),
        cost_estimate=pl.CostEstimate(flops=700_000_000, bytes_accessed=3_500_000, transcendentals=0),
        name="tile_forward",
    )(act, edge, w)


def swap_rows(x):
    return pltpu.roll(x, 4, 0)


def share_kernel(got, out):
    lane = lax.broadcasted_iota(jnp.int32, (8, I), 1)
    low = lax.broadcasted_iota(jnp.int32, (8, I), 0) < 4
    by_row = [sum(got[4 * m + x, 8:16] for x in range(4)) for m in range(8)]
    by_col = [sum(got[4 * m + x, 8:16] for m in range(8)) for x in range(4)]
    weights = sum(got[t, :8] for t in range(32))
    rest = sum(by_col)
    tails = []
    for x in range(4):
        tail = jnp.where(lane < 80, by_col[x], by_row[x])
        tail = jnp.where(lane < 96, tail, pltpu.roll(by_row[4 + x], 16, 1))
        tails.append(jnp.where(lane < 112, tail, pltpu.roll(rest, 16, 1) if x == 0 else rest))
    rows = [jnp.where(low, by_row[m], swap_rows(by_row[m + 1])) for m in range(0, 8, 2)]
    rows += [jnp.where(low, swap_rows(tails[x]), tails[x + 1]) for x in (0, 2)]
    share = jnp.concatenate(rows + [weights], axis=0).astype(BF16)
    for z in range(16):
        out[z] = share


def finish_kernel(got, ids, out):
    lane = lax.broadcasted_iota(jnp.int32, (16, I), 1)
    part = lax.broadcasted_iota(jnp.int32, (16, I), 0)
    first, last = lane < 8, lane >= 120
    z_hi = ids[0] // 2 % 2
    parts = [got[z].astype(F32) for z in range(16)]
    weights = sum(p[48:] for p in parts)
    tails = [p[32:48] for p in parts]
    edges = [sum(tails[8 * h : 8 * h + 8]) for h in range(2)]
    cols = [jnp.where(lane < 80, tails[n] + tails[8 + n], 0.0) for n in range(8)]
    body, from_low, from_high = {}, {}, {}
    for h in range(2):
        for core in range(2):
            n = 4 * h + 2 * core
            left = pltpu.roll(cols[n], I - 8, 1)
            right = pltpu.roll(cols[n + 1], 56, 1)
            body[h, core] = jnp.where(last, 0.0, left) + jnp.where(first, 0.0, right)
            from_low[h, core] = jnp.where(first, pltpu.roll(edges[h], 48 - 16 * core, 1) + right, 0.0)
            from_high[h, core] = jnp.where(last, pltpu.roll(edges[h], 32 - 16 * core, 1) + left, 0.0)
    above = jnp.where(part >= 4, pltpu.roll(from_low[1, 1], 4, 0), 0.0)
    below = jnp.where(part < 12, pltpu.roll(from_high[0, 0], 12, 0), 0.0)
    sums = {
        (0, 0): above + from_high[0, 1],
        (0, 1): from_low[0, 0] + from_high[1, 0],
        (1, 0): from_low[0, 1] + from_high[1, 1],
        (1, 1): from_low[1, 0] + below,
    }
    rest = edges[0] + edges[1]
    small = lax.broadcasted_iota(jnp.int32, (8, I), 1)
    low = lax.broadcasted_iota(jnp.int32, (8, I), 0) < 4
    rest = jnp.where(small < 112, pltpu.roll(swap_rows(rest[:8]), I - 16, 1), rest[:8])
    for core in range(2):
        rows = slice(16 * core, 16 * core + 16)
        main = [sum(p[rows] for p in parts[8 * h : 8 * h + 8]) for h in range(2)]
        total = jnp.where(
            z_hi == 0, main[0] + body[0, core] + sums[0, core], main[1] + body[1, core] + sums[1, core]
        )
        for y in range(4):
            tile = total[8 * (y // 2) : 8 * (y // 2) + 8]
            tile = jnp.where(low, tile if y % 2 == 0 else swap_rows(tile), rest)
            message = jnp.concatenate([weights, tile], axis=0).astype(BF16)
            for x in range(4):
                out[16 * core + 4 * y + x] = message


def unpack_kernel(got, gk, ge):
    parts = [got[t].astype(F32) for t in range(32)]
    main = jnp.concatenate([p[:8] for p in parts], axis=0) * (1.0 / (ROWS * I))
    low = lax.broadcasted_iota(jnp.int32, (8, I), 0) < 4
    pairs = list(zip(parts[::2], parts[1::2]))
    rest = jnp.concatenate([jnp.where(low, swap_rows(p[8:]), q[8:]) for p, q in pairs], axis=0)
    sums = jnp.concatenate([jnp.where(low, p[8:], swap_rows(q[8:])) for p, q in pairs], axis=0)
    rest = rest * (1.0 / (ROWS * I))
    ge[...] = sums.T * float(ROWS * I) ** (-0.5)
    tail = main[192:]
    for a in range(3):
        rows = slice(C * a, C * a + C)
        gk[3 * a] = main[rows, :C]
        gk[3 * a + 1] = main[rows, C:]
        if a == 2:
            gk[3 * a + 2] = tail[:, :C]
        else:
            gk[3 * a + 2] = jnp.concatenate([rest[rows, 96:], tail[:, 64 + 32 * a : 96 + 32 * a]], axis=1)


def small_call(kernel, out_shape, ids, name, **options):
    return pl.pallas_call(
        kernel,
        out_shape=out_shape,
        in_specs=[VMEM] + [SMEM] * ids,
        out_specs=jax.tree.map(lambda _: VMEM, out_shape),
        compiler_params=pltpu.CompilerParams(vmem_limit_bytes=6 * 2**20),
        cost_estimate=pl.CostEstimate(flops=1_000_000, bytes_accessed=500_000, transcendentals=0),
        name=name,
        **options,
    )


def reduce_all(parts, ids, **options):
    got = exchange(parts, PLANE_GROUPS)
    share = small_call(share_kernel, whole((16, 56, I), BF16), 0, "plane_sums", **options)(got)
    got = exchange(share, LINE_GROUPS)
    done = small_call(finish_kernel, whole((32, 16, I), BF16), 1, "line_sums", **options)(got, ids)
    got = exchange(done, PLANE_GROUPS)
    shapes = (whole((9, C, C), F32), whole((2 * C, I), F32))
    return small_call(unpack_kernel, shapes, 0, "unpack", **options)(got)


def on_device(embedding, kernel, cotangent):
    rows_local = embedding.shape[0]
    row_id = lax.axis_index("row")
    col_id = lax.axis_index("col")
    place = (col_id % 8 + sum(jnp.where(row_id % 4 == n, turn, 0) for n, turn in enumerate(TURN))) % 8
    mine = lax.dynamic_slice_in_dim(embedding, place // 2 % 2 * (J - G), J + G, 0)
    window = lax.ppermute(mine, ("row", "col"), window_pairs())
    ends = embedding.reshape(I // G, G, 2 * C)[:: I // G - 1].reshape(2 * G, 2 * C)
    ends = exchange(jnp.broadcast_to(ends[None], (ROWS,) + ends.shape), ROW_GROUPS)
    ids = jnp.stack([row_id, col_id])
    cot = cotangent.transpose(1, 2, 0)
    parts, act, edge = run_main(
        cot, kernel.reshape(9, C, C), embedding, ends, window, ids
    )
    taps = kernel.transpose(1, 3, 0, 2).reshape(192, 192)
    prediction = run_forward(act, edge, taps).transpose(2, 0, 1)
    gk, ge = reduce_all(parts, ids)
    return prediction, gk.reshape(kernel.shape), ge


def solution(mesh):
    in_specs = (P("row", None), P(), P("row", "col", None))
    out_specs = (P("row", "col", None), P(), P("row", None))
    return jax.shard_map(
        on_device, mesh=mesh, in_specs=in_specs, out_specs=out_specs, check_vma=False
    )
```

```python
import jax
import jax.numpy as jnp
from jax import lax
from jax.experimental import pallas as pl
from jax.experimental.pallas import tpu as pltpu
from jax.sharding import PartitionSpec as P

BF16 = jnp.bfloat16
F32 = jnp.float32

ROWS, COLS = 16, 32


def device_id(y, z_hi, core, x, z_lo):
    return (y * 4 + z_hi * 2 + core) * COLS + x * 8 + z_lo


PLANE_GROUPS = [
    [device_id(y, zh, k, x, zl) for k in range(2) for y in range(4) for x in range(4)]
    for zh in range(2)
    for zl in range(8)
]
LINE_GROUPS = [
    [device_id(y, zh, k, x, zl) for zh in range(2) for zl in range(8)]
    for y in range(4)
    for k in range(2)
    for x in range(4)
]
ROW_GROUPS = [
    [
        device_id(r // 4, r // 2 % 2, r % 2, x, (zl + 4 * (r // 2 % 2)) % 8)
        for r in range(ROWS)
    ]
    for x in range(4)
    for zl in range(8)
]


def window_pairs():
    pairs = []
    for row in range(ROWS):
        for col in range(COLS):
            x, z_lo = col // 8, col % 8
            place = row // 2 % 2 * 4 + col % 2 * 2 + row % 2
            source_row = col // 2
            source_col = (row // 4 + 2) % 4 * 8 + (place - TURN[z_lo // 2]) % 8
            pairs.append((source_row * COLS + source_col, row * COLS + col))
    return pairs


TURN = (0, 7, 1, 0)


def exchange(parts, groups):
    return lax.all_to_all(parts, ("row", "col"), 0, 0, axis_index_groups=groups)


C = 64
I = 128
J = 64
G = 8


def dot(a, b):
    return lax.dot_general(a, b, (((1,), (0,)), ((), ())), preferred_element_type=F32)


def dot_lanes(a, b):
    return lax.dot_general(a, b, (((1,), (1,)), ((), ())), preferred_element_type=F32)


def split_dot(x, picks):
    high = x.astype(BF16)
    low = (x - high.astype(F32)).astype(BF16)
    return dot(high, picks) + dot(low, picks)


def neighbours(value, ends, lane):
    before = jnp.where(lane < 8, ends, pltpu.roll(value, 8, 1))
    after = jnp.where(lane >= 120, ends, pltpu.roll(value, I - 8, 1))
    return before, value, after


def back_kernel(cot, w, ga, gae):
    lane = lax.broadcasted_iota(jnp.int32, (C, I), 1)
    slot = lane % 16
    weights = jnp.concatenate(
        [jnp.concatenate([w[3 * a + b] for a in range(3)], axis=1) for b in range(3)], axis=0
    )
    edge_weights = jnp.concatenate(
        [jnp.concatenate([w[b], w[6 + b]], axis=1) for b in range(3)], axis=0
    )

    def put(ref, place, value, fresh):
        ref[place] = value if fresh else ref[place] + value

    def back(k, first):
        fresh = [first, first, True]
        packed = jnp.zeros((C, I), F32)
        for p in range(0, G, 2):
            stacks = []
            for q in (p, p + 1):
                x = cot[G * k + q]
                wide = x.astype(F32)
                later = jnp.where(lane < 120, pltpu.roll(wide, I - 8, 1), 0.0).astype(BF16)
                earlier = jnp.where(lane >= 8, pltpu.roll(wide, 8, 1), 0.0).astype(BF16)
                stacks.append(jnp.concatenate([later, x, earlier], axis=0))
                packed = jnp.where(lane // 16 == q, pltpu.roll(wide, (16 * q + 8) % I, 1), packed)
            part = dot(weights, jnp.concatenate(stacks, axis=1))
            for b in range(3):
                for n, q in enumerate((p, p + 1)):
                    value = part[C * b : C * b + C, I * n : I * n + I]
                    put(ga, G * (k + b) + q, value, fresh[b])
        both = jnp.concatenate(
            [jnp.where(slot >= 8, packed, 0.0), jnp.where(slot < 8, packed, 0.0)], axis=0
        ).astype(BF16)
        part = dot(edge_weights, both)
        for b in range(3):
            put(gae, k + b, part[C * b : C * b + C], fresh[b])

    back(0, True)

    @pl.loop(1, 8)
    def _(k):
        back(k, False)


def fold8(tiles, lane):
    for step in (16, 32, 64):
        low = lane & step == 0
        tiles = [
            jnp.where(low, x, y) + pltpu.roll(jnp.where(low, y, x), step, 1)
            for x, y in zip(tiles[::2], tiles[1::2])
        ]
    return tiles[0]


def main_kernel(
    cot, ga, gae, own, ends, window, ids, out, act_out, edge_out, gk, acc, half, col_t, expand
):
    lane = lax.broadcasted_iota(jnp.int32, (C, I), 1)
    thin = lax.broadcasted_iota(jnp.int32, (16, I), 1)
    m0 = lax.broadcasted_iota(jnp.int32, (I, I), 0)
    m1 = lax.broadcasted_iota(jnp.int32, (I, I), 1)
    acc[...] = jnp.zeros_like(acc)
    gk[...] = jnp.zeros_like(gk)
    for q in range(G):
        expand[:, I * q : I * q + I] = (m0 == q).astype(BF16)
    row, col = ids[0], ids[1]
    block = col // 2
    low = ends[jnp.maximum(row - 1, 0)].astype(F32)[G:]
    high = ends[jnp.minimum(row + 1, ROWS - 1)].astype(F32)[:G]
    edge = jnp.concatenate([high, low], axis=0)
    half[:, :I] = own[...].astype(F32).T * 0.5
    half[:, I:] = jnp.concatenate([edge] * 8, axis=0).T * 0.5
    inner = window[...].astype(F32)
    low = ends[jnp.maximum(block - 1, 0)].astype(F32)[G:]
    high = ends[jnp.minimum(block + 1, ROWS - 1)].astype(F32)[:G]
    wide = jnp.where(
        col % 2 == 0, jnp.concatenate([low, inner], axis=0), jnp.concatenate([inner, high], axis=0)
    )
    col_t[...] = jnp.concatenate([wide, jnp.zeros((I - 80, I), F32)], axis=0).T

    def gate(h):
        t = jnp.tanh(h)
        p = 1.0 + t
        y = h * p
        return y, p + y * (1.0 - t)

    def group(k, taps, mask):
        spread = (m0 == G * k + m1 // 16).astype(BF16)
        gather = (m1 == G * k + m0 // 16).astype(BF16)
        wide = col_t[...]
        here = dot(wide.astype(BF16), spread)
        edge_on = jnp.where(
            lane % 16 < 8, (ids[0] < ROWS - 1).astype(F32), (ids[0] > 0).astype(F32)
        )
        if mask is not None:
            edge_on = edge_on * mask
        y, slope = gate(half[:C, I:] * here[:C] + (half[C:, I:] + 0.5 * here[C:]))
        edge_act = y * edge_on
        edge_act = edge_act.astype(BF16)
        edge_out[k] = edge_act
        g_edge = gae[k] * (slope * edge_on)
        acc[4] += g_edge * here[:C]
        acc[5] += g_edge
        near = pltpu.roll(wide, (I - G * k) % I, 1)
        near = jnp.concatenate([near[:C], near[C:] * 0.5], axis=0).astype(BF16)
        near = dot(near, expand[...])
        ends_q = [pltpu.roll(edge_act, (I - 16 * q - 8) % I, 1) for q in range(G)]
        pieces = [[[None] * 4 for _ in range(3)] for _ in range(G)]
        sums = []
        for n in range(4):
            part = slice(16 * n, 16 * n + 16)
            u_half, v_half = half[part, :I], half[C + 16 * n : C + 16 * n + 16, :I]
            row_u = row_v = 0.0
            g_u, g_v = [], []
            for q in range(G):
                uc = near[part, I * q : I * q + I]
                vc = near[C + 16 * n : C + 16 * n + 16, I * q : I * q + I]
                y, slope = gate(u_half * uc + (v_half + vc))
                g = ga[G * k + q, part] * slope
                if mask is not None:
                    y, g = y * mask, g * mask
                three = neighbours(y.astype(BF16), ends_q[q][part], thin)
                for a in range(3):
                    pieces[q][a][n] = three[a]
                act_out[G * k + q, part] = three[1]
                row_u += g * uc
                row_v += g
                g_u.append(g * u_half)
                g_v.append(g)
            acc[0, part] += row_u
            acc[1, part] += row_v
            sums.append((fold8(g_u, thin), fold8(g_v, thin)))
        for m, g in ((0, g_edge * half[:C, I:]), (1, g_edge)):
            folded = jnp.concatenate([x[m] for x in sums], axis=0) + g
            acc[2 + m] += split_dot(folded, gather)
        acts = jnp.concatenate(
            [jnp.concatenate([t for a in range(3) for t in pieces[q][a]], axis=0) for q in range(G)],
            axis=1,
        )
        cots = jnp.concatenate(
            [jnp.concatenate([cot[G * (k - b) + q] for q in range(G)], axis=1) for b in taps], axis=0
        )
        gk[:, C * taps[0] : C * (taps[-1] + 1)] += dot_lanes(acts, cots)

    group(0, [0], (col > 0).astype(F32))
    group(1, [0, 1], None)

    @pl.loop(2, 8)
    def _(k):
        group(k, [0, 1, 2], None)

    group(8, [1, 2], None)
    group(9, [2], (col < COLS - 1).astype(F32))

    def folded(x):
        x = x + pltpu.roll(x, 64, 1)
        x = x + pltpu.roll(x, 32, 1)
        return x + pltpu.roll(x, 16, 1)

    big_lane = lax.broadcasted_iota(jnp.int32, (2 * C, I), 1)
    outer = pltpu.roll(folded(jnp.concatenate([acc[4], acc[5]], axis=0)), 80, 1) * 0.5
    sums = jnp.concatenate([acc[2], acc[3] * 0.5], axis=0)
    total = gk[...]
    rest = jnp.concatenate([total[: 2 * C, 128:160]] * 4, axis=1)
    misc = jnp.where(big_lane < 80, sums, jnp.where(big_lane < 96, outer, rest))
    tail = jnp.concatenate([total[128:, 128:], total[:64, 160:], total[64:128, 160:]], axis=1)
    rows = jnp.concatenate([acc[0], acc[1]], axis=0) * 0.5
    for t in range(32):
        if t < 24:
            out[t, :8] = total[8 * t : 8 * t + 8, :128]
        else:
            out[t, :8] = tail[8 * (t - 24) : 8 * (t - 24) + 8]
        out[t, 8:12] = rows[4 * t : 4 * t + 4]
        out[t, 12:16] = misc[4 * t : 4 * t + 4]


def whole(shape, dtype):
    return jax.ShapeDtypeStruct(shape, dtype)


VMEM = pl.BlockSpec(memory_space=pltpu.VMEM)
SMEM = pl.BlockSpec(memory_space=pltpu.SMEM)


def run_back(cot, w):
    return pl.pallas_call(
        back_kernel,
        out_shape=(whole((80, C, I), F32), whole((10, C, I), F32)),
        in_specs=[VMEM, VMEM],
        out_specs=(VMEM, VMEM),
        compiler_params=pltpu.CompilerParams(vmem_limit_bytes=12 * 2**20),
        cost_estimate=pl.CostEstimate(flops=2_400_000_000, bytes_accessed=4_000_000, transcendentals=0),
        name="tile_back",
    )(cot, w)


def run_main(cot, ga, gae, own, ends, window, ids):
    return pl.pallas_call(
        main_kernel,
        out_shape=(whole((32, 16, I), F32), whole((80, C, I), BF16), whole((10, C, I), BF16)),
        in_specs=[VMEM] * 6 + [SMEM],
        out_specs=(VMEM, VMEM, VMEM),
        scratch_shapes=[
            pltpu.VMEM((192, 192), F32),
            pltpu.VMEM((6, C, I), F32),
            pltpu.VMEM((2 * C, 2 * I), F32),
            pltpu.VMEM((2 * C, I), F32),
            pltpu.VMEM((I, G * I), BF16),
        ],
        compiler_params=pltpu.CompilerParams(vmem_limit_bytes=12 * 2**20),
        cost_estimate=pl.CostEstimate(flops=1_300_000_000, bytes_accessed=6_000_000, transcendentals=700_000),
        name="tile_gradients",
    )(cot, ga, gae, own, ends, window, ids)


def forward_kernel(act, edge, w, out):
    lane = lax.broadcasted_iota(jnp.int32, (C, I), 1)
    weights = w[...]

    def group(k, taps):
        edge_act = edge[k]
        for p in range(0, G, 2):
            stacks = []
            for q in (p, p + 1):
                ends = pltpu.roll(edge_act, (I - 16 * q - 8) % I, 1)
                stacks.append(jnp.concatenate(neighbours(act[G * k + q], ends, lane), axis=0))
            stack = jnp.concatenate(stacks, axis=1)
            part = dot(weights[C * taps[0] : C * (taps[-1] + 1)], stack)
            for n, b in enumerate(taps):
                for h, q in enumerate((p, p + 1)):
                    value = part[C * n : C * n + C, I * h : I * h + I]
                    place = G * (k - b) + q
                    out[place] = value if b == 0 else out[place] + value

    group(0, [0])
    group(1, [0, 1])

    @pl.loop(2, 8)
    def _(k):
        group(k, [0, 1, 2])

    group(8, [1, 2])
    group(9, [2])


def run_forward(act, edge, w):
    return pl.pallas_call(
        forward_kernel,
        out_shape=whole((J, C, I), F32),
        in_specs=[VMEM] * 3,
        out_specs=VMEM,
        compiler_params=pltpu.CompilerParams(vmem_limit_bytes=12 * 2**20),
        cost_estimate=pl.CostEstimate(flops=700_000_000, bytes_accessed=3_500_000, transcendentals=0),
        name="tile_forward",
    )(act, edge, w)


def swap_rows(x):
    return pltpu.roll(x, 4, 0)


def share_kernel(got, out):
    lane = lax.broadcasted_iota(jnp.int32, (8, I), 1)
    low = lax.broadcasted_iota(jnp.int32, (8, I), 0) < 4
    by_row = [sum(got[4 * m + x, 8:16] for x in range(4)) for m in range(8)]
    by_col = [sum(got[4 * m + x, 8:16] for m in range(8)) for x in range(4)]
    weights = sum(got[t, :8] for t in range(32))
    rest = sum(by_col)
    tails = []
    for x in range(4):
        tail = jnp.where(lane < 80, by_col[x], by_row[x])
        tail = jnp.where(lane < 96, tail, pltpu.roll(by_row[4 + x], 16, 1))
        tails.append(jnp.where(lane < 112, tail, pltpu.roll(rest, 16, 1) if x == 0 else rest))
    rows = [jnp.where(low, by_row[m], swap_rows(by_row[m + 1])) for m in range(0, 8, 2)]
    rows += [jnp.where(low, swap_rows(tails[x]), tails[x + 1]) for x in (0, 2)]
    share = jnp.concatenate(rows + [weights], axis=0).astype(BF16)
    for z in range(16):
        out[z] = share


def finish_kernel(got, ids, out):
    lane = lax.broadcasted_iota(jnp.int32, (16, I), 1)
    part = lax.broadcasted_iota(jnp.int32, (16, I), 0)
    first, last = lane < 8, lane >= 120
    z_hi = ids[0] // 2 % 2
    parts = [got[z].astype(F32) for z in range(16)]
    weights = sum(p[48:] for p in parts)
    tails = [p[32:48] for p in parts]
    edges = [sum(tails[8 * h : 8 * h + 8]) for h in range(2)]
    cols = [jnp.where(lane < 80, tails[n] + tails[8 + n], 0.0) for n in range(8)]
    body, from_low, from_high = {}, {}, {}
    for h in range(2):
        for core in range(2):
            n = 4 * h + 2 * core
            left = pltpu.roll(cols[n], I - 8, 1)
            right = pltpu.roll(cols[n + 1], 56, 1)
            body[h, core] = jnp.where(last, 0.0, left) + jnp.where(first, 0.0, right)
            from_low[h, core] = jnp.where(first, pltpu.roll(edges[h], 48 - 16 * core, 1) + right, 0.0)
            from_high[h, core] = jnp.where(last, pltpu.roll(edges[h], 32 - 16 * core, 1) + left, 0.0)
    above = jnp.where(part >= 4, pltpu.roll(from_low[1, 1], 4, 0), 0.0)
    below = jnp.where(part < 12, pltpu.roll(from_high[0, 0], 12, 0), 0.0)
    sums = {
        (0, 0): above + from_high[0, 1],
        (0, 1): from_low[0, 0] + from_high[1, 0],
        (1, 0): from_low[0, 1] + from_high[1, 1],
        (1, 1): from_low[1, 0] + below,
    }
    rest = edges[0] + edges[1]
    small = lax.broadcasted_iota(jnp.int32, (8, I), 1)
    low = lax.broadcasted_iota(jnp.int32, (8, I), 0) < 4
    rest = jnp.where(small < 112, pltpu.roll(swap_rows(rest[:8]), I - 16, 1), rest[:8])
    for core in range(2):
        rows = slice(16 * core, 16 * core + 16)
        main = [sum(p[rows] for p in parts[8 * h : 8 * h + 8]) for h in range(2)]
        total = jnp.where(
            z_hi == 0, main[0] + body[0, core] + sums[0, core], main[1] + body[1, core] + sums[1, core]
        )
        for y in range(4):
            tile = total[8 * (y // 2) : 8 * (y // 2) + 8]
            tile = jnp.where(low, tile if y % 2 == 0 else swap_rows(tile), rest)
            message = jnp.concatenate([weights, tile], axis=0).astype(BF16)
            for x in range(4):
                out[16 * core + 4 * y + x] = message


def unpack_kernel(got, gk, ge):
    parts = [got[t].astype(F32) for t in range(32)]
    main = jnp.concatenate([p[:8] for p in parts], axis=0) * (1.0 / (ROWS * I))
    low = lax.broadcasted_iota(jnp.int32, (8, I), 0) < 4
    pairs = list(zip(parts[::2], parts[1::2]))
    rest = jnp.concatenate([jnp.where(low, swap_rows(p[8:]), q[8:]) for p, q in pairs], axis=0)
    sums = jnp.concatenate([jnp.where(low, p[8:], swap_rows(q[8:])) for p, q in pairs], axis=0)
    rest = rest * (1.0 / (ROWS * I))
    ge[...] = sums.T * float(ROWS * I) ** (-0.5)
    tail = main[192:]
    for a in range(3):
        rows = slice(C * a, C * a + C)
        gk[3 * a] = main[rows, :C]
        gk[3 * a + 1] = main[rows, C:]
        if a == 2:
            gk[3 * a + 2] = tail[:, :C]
        else:
            gk[3 * a + 2] = jnp.concatenate([rest[rows, 96:], tail[:, 64 + 32 * a : 96 + 32 * a]], axis=1)


def small_call(kernel, out_shape, ids, name, **options):
    return pl.pallas_call(
        kernel,
        out_shape=out_shape,
        in_specs=[VMEM] + [SMEM] * ids,
        out_specs=jax.tree.map(lambda _: VMEM, out_shape),
        compiler_params=pltpu.CompilerParams(vmem_limit_bytes=6 * 2**20),
        cost_estimate=pl.CostEstimate(flops=1_000_000, bytes_accessed=500_000, transcendentals=0),
        name=name,
        **options,
    )


def reduce_all(parts, ids, **options):
    got = exchange(parts, PLANE_GROUPS)
    share = small_call(share_kernel, whole((16, 56, I), BF16), 0, "plane_sums", **options)(got)
    got = exchange(share, LINE_GROUPS)
    done = small_call(finish_kernel, whole((32, 16, I), BF16), 1, "line_sums", **options)(got, ids)
    got = exchange(done, PLANE_GROUPS)
    shapes = (whole((9, C, C), F32), whole((2 * C, I), F32))
    return small_call(unpack_kernel, shapes, 0, "unpack", **options)(got)


def on_device(embedding, kernel, cotangent):
    rows_local = embedding.shape[0]
    row_id = lax.axis_index("row")
    col_id = lax.axis_index("col")
    place = (col_id % 8 + sum(jnp.where(row_id % 4 == n, turn, 0) for n, turn in enumerate(TURN))) % 8
    mine = lax.dynamic_slice_in_dim(embedding, place // 2 % 2 * (J - G), J + G, 0)
    window = lax.ppermute(mine, ("row", "col"), window_pairs())
    ends = jnp.concatenate([embedding[:G], embedding[rows_local - G :]], axis=0)
    ends = exchange(jnp.broadcast_to(ends[None], (ROWS,) + ends.shape), ROW_GROUPS)
    ids = jnp.stack([row_id, col_id])
    cot = cotangent.transpose(1, 2, 0)
    ga, gae = run_back(cot, kernel.reshape(9, C, C))
    parts, act, edge = run_main(cot, ga, gae, embedding, ends, window, ids)
    taps = kernel.transpose(1, 3, 0, 2).reshape(192, 192)
    prediction = run_forward(act, edge, taps).transpose(2, 0, 1)
    gk, ge = reduce_all(parts, ids)
    return prediction, gk.reshape(kernel.shape), ge


def solution(mesh):
    in_specs = (P("row", None), P(), P("row", "col", None))
    out_specs = (P("row", "col", None), P(), P("row", None))
    return jax.shard_map(
        on_device, mesh=mesh, in_specs=in_specs, out_specs=out_specs, check_vma=False
    )
```

```python
import jax
import jax.numpy as jnp
from jax import lax
from jax.experimental import pallas as pl
from jax.experimental.pallas import tpu as pltpu
from jax.sharding import PartitionSpec as P

BF16 = jnp.bfloat16
F32 = jnp.float32

ROWS, COLS = 16, 32


def device_id(y, z_hi, core, x, z_lo):
    return (y * 4 + z_hi * 2 + core) * COLS + x * 8 + z_lo


PLANE_GROUPS = [
    [device_id(y, zh, k, x, zl) for k in range(2) for y in range(4) for x in range(4)]
    for zh in range(2)
    for zl in range(8)
]
LINE_GROUPS = [
    [device_id(y, zh, k, x, zl) for zh in range(2) for zl in range(8)]
    for y in range(4)
    for k in range(2)
    for x in range(4)
]
ROW_GROUPS = [
    [
        device_id(r // 4, r // 2 % 2, r % 2, x, (zl + 4 * (r // 2 % 2)) % 8)
        for r in range(ROWS)
    ]
    for x in range(4)
    for zl in range(8)
]


def chip(device):
    row, col = device // COLS, device % COLS
    return col // 8, row // 4, row // 2 % 2 * 8 + col % 8


def hops(one, other):
    steps = [abs(a - b) for a, b in zip(chip(one), chip(other))]
    return sum(min(n, size - n) for n, size in zip(steps, (4, 4, 16)))


def match(sources, targets, most):
    taken = {}

    def place(target, seen):
        for source in sorted(sources, key=lambda source: hops(source, target)):
            if source in seen or hops(source, target) > most:
                continue
            seen.add(source)
            if source not in taken or place(taken[source], seen):
                taken[source] = target
                return True
        return False

    return taken if all(place(target, set()) for target in targets) else None


def window_pairs():
    pairs = []
    for block in range(ROWS):
        sources = [block * COLS + col for col in range(COLS)]
        targets = [row * COLS + 2 * block + half for row in range(ROWS) for half in range(2)]
        found = next(filter(None, (match(sources, targets, most) for most in range(13))))
        pairs += sorted(found.items())
    return pairs


def exchange(parts, groups):
    return lax.all_to_all(parts, ("row", "col"), 0, 0, axis_index_groups=groups)


C = 64
I = 128
J = 64
G = 8


def dot(a, b):
    return lax.dot_general(a, b, (((1,), (0,)), ((), ())), preferred_element_type=F32)


def dot_lanes(a, b):
    return lax.dot_general(a, b, (((1,), (1,)), ((), ())), preferred_element_type=F32)


def split_dot(x, picks):
    high = x.astype(BF16)
    low = (x - high.astype(F32)).astype(BF16)
    return dot(high, picks) + dot(low, picks)


def neighbours(value, ends, lane):
    before = jnp.where(lane < 8, ends, pltpu.roll(value, 8, 1))
    after = jnp.where(lane >= 120, ends, pltpu.roll(value, I - 8, 1))
    return before, value, after


def back_kernel(cot, w, ga, gae):
    lane = lax.broadcasted_iota(jnp.int32, (C, I), 1)
    slot = lane % 16
    weights = jnp.concatenate(
        [jnp.concatenate([w[3 * a + b] for a in range(3)], axis=1) for b in range(3)], axis=0
    )
    edge_weights = jnp.concatenate(
        [jnp.concatenate([w[b], w[6 + b]], axis=1) for b in range(3)], axis=0
    )

    def put(ref, place, value, fresh):
        ref[place] = value if fresh else ref[place] + value

    def back(k, first):
        fresh = [first, first, True]
        packed = jnp.zeros((C, I), F32)
        for p in range(0, G, 2):
            stacks = []
            for q in (p, p + 1):
                x = cot[G * k + q]
                wide = x.astype(F32)
                later = jnp.where(lane < 120, pltpu.roll(wide, I - 8, 1), 0.0).astype(BF16)
                earlier = jnp.where(lane >= 8, pltpu.roll(wide, 8, 1), 0.0).astype(BF16)
                stacks.append(jnp.concatenate([later, x, earlier], axis=0))
                packed = jnp.where(lane // 16 == q, pltpu.roll(wide, (16 * q + 8) % I, 1), packed)
            part = dot(weights, jnp.concatenate(stacks, axis=1))
            for b in range(3):
                for n, q in enumerate((p, p + 1)):
                    value = part[C * b : C * b + C, I * n : I * n + I]
                    put(ga, G * (k + b) + q, value, fresh[b])
        both = jnp.concatenate(
            [jnp.where(slot >= 8, packed, 0.0), jnp.where(slot < 8, packed, 0.0)], axis=0
        ).astype(BF16)
        part = dot(edge_weights, both)
        for b in range(3):
            put(gae, k + b, part[C * b : C * b + C], fresh[b])

    back(0, True)

    @pl.loop(1, 8)
    def _(k):
        back(k, False)


def fold8(tiles, lane):
    for step in (16, 32, 64):
        low = lane & step == 0
        tiles = [
            jnp.where(low, x, y) + pltpu.roll(jnp.where(low, y, x), step, 1)
            for x, y in zip(tiles[::2], tiles[1::2])
        ]
    return tiles[0]


def main_kernel(
    cot, ga, gae, own, ends, window, ids, out, act_out, edge_out, gk, acc, half, col_t, expand
):
    lane = lax.broadcasted_iota(jnp.int32, (C, I), 1)
    thin = lax.broadcasted_iota(jnp.int32, (16, I), 1)
    m0 = lax.broadcasted_iota(jnp.int32, (I, I), 0)
    m1 = lax.broadcasted_iota(jnp.int32, (I, I), 1)
    acc[...] = jnp.zeros_like(acc)
    gk[...] = jnp.zeros_like(gk)
    for q in range(G):
        expand[:, I * q : I * q + I] = (m0 == q).astype(BF16)
    row, col = ids[0], ids[1]
    block = col // 2
    low = ends[jnp.maximum(row - 1, 0)].astype(F32)[G:]
    high = ends[jnp.minimum(row + 1, ROWS - 1)].astype(F32)[:G]
    edge = jnp.concatenate([high, low], axis=0)
    half[:, :I] = own[...].astype(F32).T * 0.5
    half[:, I:] = jnp.concatenate([edge] * 8, axis=0).T * 0.5
    inner = window[...].astype(F32)
    inner = jnp.where(col % 2 == 0, inner[: J + G], inner[J - G :])
    low = ends[jnp.maximum(block - 1, 0)].astype(F32)[G:]
    high = ends[jnp.minimum(block + 1, ROWS - 1)].astype(F32)[:G]
    wide = jnp.where(
        col % 2 == 0, jnp.concatenate([low, inner], axis=0), jnp.concatenate([inner, high], axis=0)
    )
    col_t[...] = jnp.concatenate([wide, jnp.zeros((I - 80, I), F32)], axis=0).T

    def gate(h):
        t = jnp.tanh(h)
        p = 1.0 + t
        y = h * p
        return y, p + y * (1.0 - t)

    def group(k, taps, mask):
        spread = (m0 == G * k + m1 // 16).astype(BF16)
        gather = (m1 == G * k + m0 // 16).astype(BF16)
        wide = col_t[...]
        here = dot(wide.astype(BF16), spread)
        edge_on = jnp.where(
            lane % 16 < 8, (ids[0] < ROWS - 1).astype(F32), (ids[0] > 0).astype(F32)
        )
        if mask is not None:
            edge_on = edge_on * mask
        y, slope = gate(half[:C, I:] * here[:C] + (half[C:, I:] + 0.5 * here[C:]))
        edge_act = y * edge_on
        edge_act = edge_act.astype(BF16)
        edge_out[k] = edge_act
        g_edge = gae[k] * (slope * edge_on)
        acc[4] += g_edge * here[:C]
        acc[5] += g_edge
        near = pltpu.roll(wide, (I - G * k) % I, 1)
        near = jnp.concatenate([near[:C], near[C:] * 0.5], axis=0).astype(BF16)
        near = dot(near, expand[...])
        ends_q = [pltpu.roll(edge_act, (I - 16 * q - 8) % I, 1) for q in range(G)]
        pieces = [[[None] * 4 for _ in range(3)] for _ in range(G)]
        sums = []
        for n in range(4):
            part = slice(16 * n, 16 * n + 16)
            u_half, v_half = half[part, :I], half[C + 16 * n : C + 16 * n + 16, :I]
            row_u = row_v = 0.0
            g_u, g_v = [], []
            for q in range(G):
                uc = near[part, I * q : I * q + I]
                vc = near[C + 16 * n : C + 16 * n + 16, I * q : I * q + I]
                y, slope = gate(u_half * uc + (v_half + vc))
                g = ga[G * k + q, part] * slope
                if mask is not None:
                    y, g = y * mask, g * mask
                three = neighbours(y.astype(BF16), ends_q[q][part], thin)
                for a in range(3):
                    pieces[q][a][n] = three[a]
                act_out[G * k + q, part] = three[1]
                row_u += g * uc
                row_v += g
                g_u.append(g * u_half)
                g_v.append(g)
            acc[0, part] += row_u
            acc[1, part] += row_v
            sums.append((fold8(g_u, thin), fold8(g_v, thin)))
        for m, g in ((0, g_edge * half[:C, I:]), (1, g_edge)):
            folded = jnp.concatenate([x[m] for x in sums], axis=0) + g
            acc[2 + m] += split_dot(folded, gather)
        acts = jnp.concatenate(
            [jnp.concatenate([t for a in range(3) for t in pieces[q][a]], axis=0) for q in range(G)],
            axis=1,
        )
        cots = jnp.concatenate(
            [jnp.concatenate([cot[G * (k - b) + q] for q in range(G)], axis=1) for b in taps], axis=0
        )
        gk[:, C * taps[0] : C * (taps[-1] + 1)] += dot_lanes(acts, cots)

    group(0, [0], (col > 0).astype(F32))
    group(1, [0, 1], None)

    @pl.loop(2, 8)
    def _(k):
        group(k, [0, 1, 2], None)

    group(8, [1, 2], None)
    group(9, [2], (col < COLS - 1).astype(F32))

    def folded(x):
        x = x + pltpu.roll(x, 64, 1)
        x = x + pltpu.roll(x, 32, 1)
        return x + pltpu.roll(x, 16, 1)

    big_lane = lax.broadcasted_iota(jnp.int32, (2 * C, I), 1)
    outer = pltpu.roll(folded(jnp.concatenate([acc[4], acc[5]], axis=0)), 80, 1) * 0.5
    sums = jnp.concatenate([acc[2], acc[3] * 0.5], axis=0)
    total = gk[...]
    rest = jnp.concatenate([total[: 2 * C, 128:160]] * 4, axis=1)
    misc = jnp.where(big_lane < 80, sums, jnp.where(big_lane < 96, outer, rest))
    tail = jnp.concatenate([total[128:, 128:], total[:64, 160:], total[64:128, 160:]], axis=1)
    rows = jnp.concatenate([acc[0], acc[1]], axis=0) * 0.5
    for t in range(32):
        if t < 24:
            out[t, :8] = total[8 * t : 8 * t + 8, :128]
        else:
            out[t, :8] = tail[8 * (t - 24) : 8 * (t - 24) + 8]
        out[t, 8:12] = rows[4 * t : 4 * t + 4]
        out[t, 12:16] = misc[4 * t : 4 * t + 4]


def whole(shape, dtype):
    return jax.ShapeDtypeStruct(shape, dtype)


VMEM = pl.BlockSpec(memory_space=pltpu.VMEM)
SMEM = pl.BlockSpec(memory_space=pltpu.SMEM)


def run_back(cot, w):
    return pl.pallas_call(
        back_kernel,
        out_shape=(whole((80, C, I), F32), whole((10, C, I), F32)),
        in_specs=[VMEM, VMEM],
        out_specs=(VMEM, VMEM),
        compiler_params=pltpu.CompilerParams(vmem_limit_bytes=12 * 2**20),
        cost_estimate=pl.CostEstimate(flops=2_400_000_000, bytes_accessed=4_000_000, transcendentals=0),
        name="tile_back",
    )(cot, w)


def run_main(cot, ga, gae, own, ends, window, ids):
    return pl.pallas_call(
        main_kernel,
        out_shape=(whole((32, 16, I), F32), whole((80, C, I), BF16), whole((10, C, I), BF16)),
        in_specs=[VMEM] * 6 + [SMEM],
        out_specs=(VMEM, VMEM, VMEM),
        scratch_shapes=[
            pltpu.VMEM((192, 192), F32),
            pltpu.VMEM((6, C, I), F32),
            pltpu.VMEM((2 * C, 2 * I), F32),
            pltpu.VMEM((2 * C, I), F32),
            pltpu.VMEM((I, G * I), BF16),
        ],
        compiler_params=pltpu.CompilerParams(vmem_limit_bytes=12 * 2**20),
        cost_estimate=pl.CostEstimate(flops=1_300_000_000, bytes_accessed=6_000_000, transcendentals=700_000),
        name="tile_gradients",
    )(cot, ga, gae, own, ends, window, ids)


def forward_kernel(act, edge, w, out):
    lane = lax.broadcasted_iota(jnp.int32, (C, I), 1)
    weights = w[...]

    def group(k, taps):
        edge_act = edge[k]
        for p in range(0, G, 2):
            stacks = []
            for q in (p, p + 1):
                ends = pltpu.roll(edge_act, (I - 16 * q - 8) % I, 1)
                stacks.append(jnp.concatenate(neighbours(act[G * k + q], ends, lane), axis=0))
            stack = jnp.concatenate(stacks, axis=1)
            part = dot(weights[C * taps[0] : C * (taps[-1] + 1)], stack)
            for n, b in enumerate(taps):
                for h, q in enumerate((p, p + 1)):
                    value = part[C * n : C * n + C, I * h : I * h + I]
                    place = G * (k - b) + q
                    out[place] = value if b == 0 else out[place] + value

    group(0, [0])
    group(1, [0, 1])

    @pl.loop(2, 8)
    def _(k):
        group(k, [0, 1, 2])

    group(8, [1, 2])
    group(9, [2])


def run_forward(act, edge, w):
    return pl.pallas_call(
        forward_kernel,
        out_shape=whole((J, C, I), F32),
        in_specs=[VMEM] * 3,
        out_specs=VMEM,
        compiler_params=pltpu.CompilerParams(vmem_limit_bytes=12 * 2**20),
        cost_estimate=pl.CostEstimate(flops=700_000_000, bytes_accessed=3_500_000, transcendentals=0),
        name="tile_forward",
    )(act, edge, w)


def swap_rows(x):
    return pltpu.roll(x, 4, 0)


def share_kernel(got, out):
    lane = lax.broadcasted_iota(jnp.int32, (8, I), 1)
    low = lax.broadcasted_iota(jnp.int32, (8, I), 0) < 4
    by_row = [sum(got[4 * m + x, 8:16] for x in range(4)) for m in range(8)]
    by_col = [sum(got[4 * m + x, 8:16] for m in range(8)) for x in range(4)]
    weights = sum(got[t, :8] for t in range(32))
    rest = sum(by_col)
    tails = []
    for x in range(4):
        tail = jnp.where(lane < 80, by_col[x], by_row[x])
        tail = jnp.where(lane < 96, tail, pltpu.roll(by_row[4 + x], 16, 1))
        tails.append(jnp.where(lane < 112, tail, pltpu.roll(rest, 16, 1) if x == 0 else rest))
    rows = [jnp.where(low, by_row[m], swap_rows(by_row[m + 1])) for m in range(0, 8, 2)]
    rows += [jnp.where(low, swap_rows(tails[x]), tails[x + 1]) for x in (0, 2)]
    share = jnp.concatenate(rows + [weights], axis=0).astype(BF16)
    for z in range(16):
        out[z] = share


def finish_kernel(got, ids, out):
    lane = lax.broadcasted_iota(jnp.int32, (16, I), 1)
    part = lax.broadcasted_iota(jnp.int32, (16, I), 0)
    first, last = lane < 8, lane >= 120
    z_hi = ids[0] // 2 % 2
    parts = [got[z].astype(F32) for z in range(16)]
    weights = sum(p[48:] for p in parts)
    tails = [p[32:48] for p in parts]
    edges = [sum(tails[8 * h : 8 * h + 8]) for h in range(2)]
    cols = [jnp.where(lane < 80, tails[n] + tails[8 + n], 0.0) for n in range(8)]
    body, from_low, from_high = {}, {}, {}
    for h in range(2):
        for core in range(2):
            n = 4 * h + 2 * core
            left = pltpu.roll(cols[n], I - 8, 1)
            right = pltpu.roll(cols[n + 1], 56, 1)
            body[h, core] = jnp.where(last, 0.0, left) + jnp.where(first, 0.0, right)
            from_low[h, core] = jnp.where(first, pltpu.roll(edges[h], 48 - 16 * core, 1) + right, 0.0)
            from_high[h, core] = jnp.where(last, pltpu.roll(edges[h], 32 - 16 * core, 1) + left, 0.0)
    above = jnp.where(part >= 4, pltpu.roll(from_low[1, 1], 4, 0), 0.0)
    below = jnp.where(part < 12, pltpu.roll(from_high[0, 0], 12, 0), 0.0)
    sums = {
        (0, 0): above + from_high[0, 1],
        (0, 1): from_low[0, 0] + from_high[1, 0],
        (1, 0): from_low[0, 1] + from_high[1, 1],
        (1, 1): from_low[1, 0] + below,
    }
    rest = edges[0] + edges[1]
    small = lax.broadcasted_iota(jnp.int32, (8, I), 1)
    low = lax.broadcasted_iota(jnp.int32, (8, I), 0) < 4
    rest = jnp.where(small < 112, pltpu.roll(swap_rows(rest[:8]), I - 16, 1), rest[:8])
    for core in range(2):
        rows = slice(16 * core, 16 * core + 16)
        main = [sum(p[rows] for p in parts[8 * h : 8 * h + 8]) for h in range(2)]
        total = jnp.where(
            z_hi == 0, main[0] + body[0, core] + sums[0, core], main[1] + body[1, core] + sums[1, core]
        )
        for y in range(4):
            tile = total[8 * (y // 2) : 8 * (y // 2) + 8]
            tile = jnp.where(low, tile if y % 2 == 0 else swap_rows(tile), rest)
            message = jnp.concatenate([weights, tile], axis=0).astype(BF16)
            for x in range(4):
                out[16 * core + 4 * y + x] = message


def unpack_kernel(got, gk, ge):
    parts = [got[t].astype(F32) for t in range(32)]
    main = jnp.concatenate([p[:8] for p in parts], axis=0) * (1.0 / (ROWS * I))
    low = lax.broadcasted_iota(jnp.int32, (8, I), 0) < 4
    pairs = list(zip(parts[::2], parts[1::2]))
    rest = jnp.concatenate([jnp.where(low, swap_rows(p[8:]), q[8:]) for p, q in pairs], axis=0)
    sums = jnp.concatenate([jnp.where(low, p[8:], swap_rows(q[8:])) for p, q in pairs], axis=0)
    rest = rest * (1.0 / (ROWS * I))
    ge[...] = sums.T * float(ROWS * I) ** (-0.5)
    tail = main[192:]
    for a in range(3):
        rows = slice(C * a, C * a + C)
        gk[3 * a] = main[rows, :C]
        gk[3 * a + 1] = main[rows, C:]
        if a == 2:
            gk[3 * a + 2] = tail[:, :C]
        else:
            gk[3 * a + 2] = jnp.concatenate([rest[rows, 96:], tail[:, 64 + 32 * a : 96 + 32 * a]], axis=1)


def small_call(kernel, out_shape, ids, name, **options):
    return pl.pallas_call(
        kernel,
        out_shape=out_shape,
        in_specs=[VMEM] + [SMEM] * ids,
        out_specs=jax.tree.map(lambda _: VMEM, out_shape),
        compiler_params=pltpu.CompilerParams(vmem_limit_bytes=6 * 2**20),
        cost_estimate=pl.CostEstimate(flops=1_000_000, bytes_accessed=500_000, transcendentals=0),
        name=name,
        **options,
    )


def reduce_all(parts, ids, **options):
    got = exchange(parts, PLANE_GROUPS)
    share = small_call(share_kernel, whole((16, 56, I), BF16), 0, "plane_sums", **options)(got)
    got = exchange(share, LINE_GROUPS)
    done = small_call(finish_kernel, whole((32, 16, I), BF16), 1, "line_sums", **options)(got, ids)
    got = exchange(done, PLANE_GROUPS)
    shapes = (whole((9, C, C), F32), whole((2 * C, I), F32))
    return small_call(unpack_kernel, shapes, 0, "unpack", **options)(got)


def on_device(embedding, kernel, cotangent):
    rows_local = embedding.shape[0]
    row_id = lax.axis_index("row")
    col_id = lax.axis_index("col")
    window = lax.ppermute(embedding, ("row", "col"), window_pairs())
    ends = jnp.concatenate([embedding[:G], embedding[rows_local - G :]], axis=0)
    ends = exchange(jnp.broadcast_to(ends[None], (ROWS,) + ends.shape), ROW_GROUPS)
    ids = jnp.stack([row_id, col_id])
    cot = cotangent.transpose(1, 2, 0)
    ga, gae = run_back(cot, kernel.reshape(9, C, C))
    parts, act, edge = run_main(cot, ga, gae, embedding, ends, window, ids)
    taps = kernel.transpose(1, 3, 0, 2).reshape(192, 192)
    prediction = run_forward(act, edge, taps).transpose(2, 0, 1)
    gk, ge = reduce_all(parts, ids)
    return prediction, gk.reshape(kernel.shape), ge


def solution(mesh):
    in_specs = (P("row", None), P(), P("row", "col", None))
    out_specs = (P("row", "col", None), P(), P("row", None))
    return jax.shard_map(
        on_device, mesh=mesh, in_specs=in_specs, out_specs=out_specs, check_vma=False
    )
```

```python
import jax
import jax.numpy as jnp
from jax import lax
from jax.experimental import pallas as pl
from jax.experimental.pallas import tpu as pltpu
from jax.sharding import PartitionSpec as P

BF16 = jnp.bfloat16
F32 = jnp.float32

ROWS, COLS = 16, 32


def device_id(y, z_hi, core, x, z_lo):
    return (y * 4 + z_hi * 2 + core) * COLS + x * 8 + z_lo


PLANE_GROUPS = [
    [device_id(y, zh, k, x, zl) for k in range(2) for y in range(4) for x in range(4)]
    for zh in range(2)
    for zl in range(8)
]
LINE_GROUPS = [
    [device_id(y, zh, k, x, zl) for zh in range(2) for zl in range(8)]
    for y in range(4)
    for k in range(2)
    for x in range(4)
]
ROW_GROUPS = [
    [
        device_id(r // 4, r // 2 % 2, r % 2, x, (zl + 4 * (r // 2 % 2)) % 8)
        for r in range(ROWS)
    ]
    for x in range(4)
    for zl in range(8)
]


def window_pairs():
    pairs = []
    for row in range(ROWS):
        for col in range(COLS):
            x, z_lo = col // 8, col % 8
            place = row // 2 % 2 * 4 + col % 2 * 2 + row % 2
            source_row = col // 2
            source_col = (row // 4 + 2) % 4 * 8 + (place - TURN[z_lo // 2]) % 8
            pairs.append((source_row * COLS + source_col, row * COLS + col))
    return pairs


TURN = (0, 7, 1, 0)


def exchange(parts, groups):
    return lax.all_to_all(parts, ("row", "col"), 0, 0, axis_index_groups=groups)


C = 64
I = 128
J = 64
G = 8


def dot(a, b):
    return lax.dot_general(a, b, (((1,), (0,)), ((), ())), preferred_element_type=F32)


def dot_lanes(a, b):
    return lax.dot_general(a, b, (((1,), (1,)), ((), ())), preferred_element_type=F32)


def split_dot(x, picks):
    high = x.astype(BF16)
    low = (x - high.astype(F32)).astype(BF16)
    return dot(high, picks) + dot(low, picks)


def neighbours(value, ends, lane):
    before = jnp.where(lane < 8, ends, pltpu.roll(value, 8, 1))
    after = jnp.where(lane >= 120, ends, pltpu.roll(value, I - 8, 1))
    return before, value, after


def back_kernel(cot, w, ga, gae):
    lane = lax.broadcasted_iota(jnp.int32, (C, I), 1)
    slot = lane % 16
    weights = jnp.concatenate(
        [jnp.concatenate([w[3 * a + b] for a in range(3)], axis=1) for b in range(3)], axis=0
    )
    edge_weights = jnp.concatenate(
        [jnp.concatenate([w[b], w[6 + b]], axis=1) for b in range(3)], axis=0
    )

    def put(ref, place, value, fresh):
        ref[place] = value if fresh else ref[place] + value

    def back(k, first):
        fresh = [first, first, True]
        packed = jnp.zeros((C, I), F32)
        for p in range(0, G, 2):
            stacks = []
            for q in (p, p + 1):
                x = cot[G * k + q]
                wide = x.astype(F32)
                later = jnp.where(lane < 120, pltpu.roll(wide, I - 8, 1), 0.0).astype(BF16)
                earlier = jnp.where(lane >= 8, pltpu.roll(wide, 8, 1), 0.0).astype(BF16)
                stacks.append(jnp.concatenate([later, x, earlier], axis=0))
                packed = jnp.where(lane // 16 == q, pltpu.roll(wide, (16 * q + 8) % I, 1), packed)
            part = dot(weights, jnp.concatenate(stacks, axis=1))
            for b in range(3):
                for n, q in enumerate((p, p + 1)):
                    value = part[C * b : C * b + C, I * n : I * n + I]
                    put(ga, G * (k + b) + q, value, fresh[b])
        both = jnp.concatenate(
            [jnp.where(slot >= 8, packed, 0.0), jnp.where(slot < 8, packed, 0.0)], axis=0
        ).astype(BF16)
        part = dot(edge_weights, both)
        for b in range(3):
            put(gae, k + b, part[C * b : C * b + C], fresh[b])

    back(0, True)

    @pl.loop(1, 8)
    def _(k):
        back(k, False)


def fold8(tiles, lane):
    for step in (16, 32, 64):
        low = lane & step == 0
        tiles = [
            jnp.where(low, x, y) + pltpu.roll(jnp.where(low, y, x), step, 1)
            for x, y in zip(tiles[::2], tiles[1::2])
        ]
    return tiles[0]


def main_kernel(
    cot, ga, gae, own, ends, window, ids, out, act_out, edge_out, gk, acc, half, col_t, expand
):
    lane = lax.broadcasted_iota(jnp.int32, (C, I), 1)
    thin = lax.broadcasted_iota(jnp.int32, (16, I), 1)
    m0 = lax.broadcasted_iota(jnp.int32, (I, I), 0)
    m1 = lax.broadcasted_iota(jnp.int32, (I, I), 1)
    acc[...] = jnp.zeros_like(acc)
    gk[...] = jnp.zeros_like(gk)
    for q in range(G):
        expand[:, I * q : I * q + I] = (m0 == q).astype(BF16)
    row, col = ids[0], ids[1]
    block = col // 2
    low = ends[jnp.maximum(row - 1, 0)].astype(F32)[G:]
    high = ends[jnp.minimum(row + 1, ROWS - 1)].astype(F32)[:G]
    edge = jnp.concatenate([high, low], axis=0)
    half[:, :I] = own[...].astype(F32).T * 0.5
    half[:, I:] = jnp.concatenate([edge] * 8, axis=0).T * 0.5
    inner = window[...].astype(F32)
    low = ends[jnp.maximum(block - 1, 0)].astype(F32)[G:]
    high = ends[jnp.minimum(block + 1, ROWS - 1)].astype(F32)[:G]
    wide = jnp.where(
        col % 2 == 0, jnp.concatenate([low, inner], axis=0), jnp.concatenate([inner, high], axis=0)
    )
    col_t[...] = jnp.concatenate([wide, jnp.zeros((I - 80, I), F32)], axis=0).T

    def gate(h):
        t = jnp.tanh(h)
        p = 1.0 + t
        y = h * p
        return y, p + y * (1.0 - t)

    def group(k, taps, mask):
        spread = (m0 == G * k + m1 // 16).astype(BF16)
        gather = (m1 == G * k + m0 // 16).astype(BF16)
        wide = col_t[...]
        here = dot(wide.astype(BF16), spread)
        edge_on = jnp.where(
            lane % 16 < 8, (ids[0] < ROWS - 1).astype(F32), (ids[0] > 0).astype(F32)
        )
        if mask is not None:
            edge_on = edge_on * mask
        y, slope = gate(half[:C, I:] * here[:C] + (half[C:, I:] + 0.5 * here[C:]))
        edge_act = y * edge_on
        edge_act = edge_act.astype(BF16)
        edge_out[k] = edge_act
        g_edge = gae[k] * (slope * edge_on)
        acc[4] += g_edge * here[:C]
        acc[5] += g_edge
        near = pltpu.roll(wide, (I - G * k) % I, 1)
        near = jnp.concatenate([near[:C], near[C:] * 0.5], axis=0).astype(BF16)
        near = dot(near, expand[...])
        ends_q = [pltpu.roll(edge_act, (I - 16 * q - 8) % I, 1) for q in range(G)]
        pieces = [[[None] * 4 for _ in range(3)] for _ in range(G)]
        sums = []
        for n in range(4):
            part = slice(16 * n, 16 * n + 16)
            u_half, v_half = half[part, :I], half[C + 16 * n : C + 16 * n + 16, :I]
            row_u = row_v = 0.0
            g_u, g_v = [], []
            for q in range(G):
                uc = near[part, I * q : I * q + I]
                vc = near[C + 16 * n : C + 16 * n + 16, I * q : I * q + I]
                y, slope = gate(u_half * uc + (v_half + vc))
                g = ga[G * k + q, part] * slope
                if mask is not None:
                    y, g = y * mask, g * mask
                three = neighbours(y.astype(BF16), ends_q[q][part], thin)
                for a in range(3):
                    pieces[q][a][n] = three[a]
                act_out[G * k + q, part] = three[1]
                row_u += g * uc
                row_v += g
                g_u.append(g * u_half)
                g_v.append(g)
            acc[0, part] += row_u
            acc[1, part] += row_v
            sums.append((fold8(g_u, thin), fold8(g_v, thin)))
        for m, g in ((0, g_edge * half[:C, I:]), (1, g_edge)):
            folded = jnp.concatenate([x[m] for x in sums], axis=0) + g
            acc[2 + m] += split_dot(folded, gather)
        acts = jnp.concatenate(
            [jnp.concatenate([t for a in range(3) for t in pieces[q][a]], axis=0) for q in range(G)],
            axis=1,
        )
        cots = jnp.concatenate(
            [jnp.concatenate([cot[G * (k - b) + q] for q in range(G)], axis=1) for b in taps], axis=0
        )
        gk[:, C * taps[0] : C * (taps[-1] + 1)] += dot_lanes(acts, cots)

    group(0, [0], (col > 0).astype(F32))
    group(1, [0, 1], None)

    @pl.loop(2, 8)
    def _(k):
        group(k, [0, 1, 2], None)

    group(8, [1, 2], None)
    group(9, [2], (col < COLS - 1).astype(F32))

    def folded(x):
        x = x + pltpu.roll(x, 64, 1)
        x = x + pltpu.roll(x, 32, 1)
        return x + pltpu.roll(x, 16, 1)

    big_lane = lax.broadcasted_iota(jnp.int32, (2 * C, I), 1)
    outer = pltpu.roll(folded(jnp.concatenate([acc[4], acc[5]], axis=0)), 80, 1) * 0.5
    sums = jnp.concatenate([acc[2], acc[3] * 0.5], axis=0)
    total = gk[...]
    rest = jnp.concatenate([total[: 2 * C, 128:160]] * 4, axis=1)
    misc = jnp.where(big_lane < 80, sums, jnp.where(big_lane < 96, outer, rest))
    tail = jnp.concatenate([total[128:, 128:], total[:64, 160:], total[64:128, 160:]], axis=1)
    rows = jnp.concatenate([acc[0], acc[1]], axis=0) * 0.5
    for t in range(32):
        if t < 24:
            out[t, :8] = total[8 * t : 8 * t + 8, :128]
        else:
            out[t, :8] = tail[8 * (t - 24) : 8 * (t - 24) + 8]
        out[t, 8:12] = rows[4 * t : 4 * t + 4]
        out[t, 12:16] = misc[4 * t : 4 * t + 4]


def whole(shape, dtype):
    return jax.ShapeDtypeStruct(shape, dtype)


VMEM = pl.BlockSpec(memory_space=pltpu.VMEM)
SMEM = pl.BlockSpec(memory_space=pltpu.SMEM)


def run_back(cot, w):
    return pl.pallas_call(
        back_kernel,
        out_shape=(whole((80, C, I), F32), whole((10, C, I), F32)),
        in_specs=[VMEM, VMEM],
        out_specs=(VMEM, VMEM),
        compiler_params=pltpu.CompilerParams(vmem_limit_bytes=12 * 2**20),
        cost_estimate=pl.CostEstimate(flops=2_400_000_000, bytes_accessed=4_000_000, transcendentals=0),
        name="tile_back",
    )(cot, w)


def run_main(cot, ga, gae, own, ends, window, ids):
    return pl.pallas_call(
        main_kernel,
        out_shape=(whole((32, 16, I), F32), whole((80, C, I), BF16), whole((10, C, I), BF16)),
        in_specs=[VMEM] * 6 + [SMEM],
        out_specs=(VMEM, VMEM, VMEM),
        scratch_shapes=[
            pltpu.VMEM((192, 192), F32),
            pltpu.VMEM((6, C, I), F32),
            pltpu.VMEM((2 * C, 2 * I), F32),
            pltpu.VMEM((2 * C, I), F32),
            pltpu.VMEM((I, G * I), BF16),
        ],
        compiler_params=pltpu.CompilerParams(vmem_limit_bytes=12 * 2**20),
        cost_estimate=pl.CostEstimate(flops=1_300_000_000, bytes_accessed=6_000_000, transcendentals=700_000),
        name="tile_gradients",
    )(cot, ga, gae, own, ends, window, ids)


def forward_kernel(act, edge, w, out):
    lane = lax.broadcasted_iota(jnp.int32, (C, I), 1)
    weights = w[...]

    def group(k, taps):
        edge_act = edge[k]
        for p in range(0, G, 2):
            stacks = []
            for q in (p, p + 1):
                ends = pltpu.roll(edge_act, (I - 16 * q - 8) % I, 1)
                stacks.append(jnp.concatenate(neighbours(act[G * k + q], ends, lane), axis=0))
            stack = jnp.concatenate(stacks, axis=1)
            part = dot(weights[C * taps[0] : C * (taps[-1] + 1)], stack)
            for n, b in enumerate(taps):
                for h, q in enumerate((p, p + 1)):
                    value = part[C * n : C * n + C, I * h : I * h + I]
                    place = G * (k - b) + q
                    out[place] = value if b == 0 else out[place] + value

    group(0, [0])
    group(1, [0, 1])

    @pl.loop(2, 8)
    def _(k):
        group(k, [0, 1, 2])

    group(8, [1, 2])
    group(9, [2])


def run_forward(act, edge, w):
    return pl.pallas_call(
        forward_kernel,
        out_shape=whole((J, C, I), F32),
        in_specs=[VMEM] * 3,
        out_specs=VMEM,
        compiler_params=pltpu.CompilerParams(vmem_limit_bytes=12 * 2**20),
        cost_estimate=pl.CostEstimate(flops=700_000_000, bytes_accessed=3_500_000, transcendentals=0),
        name="tile_forward",
    )(act, edge, w)


def swap_rows(x):
    return pltpu.roll(x, 4, 0)


def share_kernel(got, out):
    lane = lax.broadcasted_iota(jnp.int32, (8, I), 1)
    low = lax.broadcasted_iota(jnp.int32, (8, I), 0) < 4
    by_row = [sum(got[4 * m + x, 8:16] for x in range(4)) for m in range(8)]
    by_col = [sum(got[4 * m + x, 8:16] for m in range(8)) for x in range(4)]
    weights = sum(got[t, :8] for t in range(32))
    rest = sum(by_col)
    tails = []
    for x in range(4):
        tail = jnp.where(lane < 80, by_col[x], by_row[x])
        tail = jnp.where(lane < 96, tail, pltpu.roll(by_row[4 + x], 16, 1))
        tails.append(jnp.where(lane < 112, tail, pltpu.roll(rest, 16, 1) if x == 0 else rest))
    rows = [jnp.where(low, by_row[m], swap_rows(by_row[m + 1])) for m in range(0, 8, 2)]
    rows += [jnp.where(low, swap_rows(tails[x]), tails[x + 1]) for x in (0, 2)]
    share = jnp.concatenate(rows + [weights], axis=0).astype(BF16)
    for z in range(16):
        out[z] = share


def finish_kernel(got, ids, out):
    lane = lax.broadcasted_iota(jnp.int32, (16, I), 1)
    part = lax.broadcasted_iota(jnp.int32, (16, I), 0)
    first, last = lane < 8, lane >= 120
    z_hi = ids[0] // 2 % 2
    parts = [got[z].astype(F32) for z in range(16)]
    weights = sum(p[48:] for p in parts)
    tails = [p[32:48] for p in parts]
    edges = [sum(tails[8 * h : 8 * h + 8]) for h in range(2)]
    cols = [jnp.where(lane < 80, tails[n] + tails[8 + n], 0.0) for n in range(8)]
    body, from_low, from_high = {}, {}, {}
    for h in range(2):
        for core in range(2):
            n = 4 * h + 2 * core
            left = pltpu.roll(cols[n], I - 8, 1)
            right = pltpu.roll(cols[n + 1], 56, 1)
            body[h, core] = jnp.where(last, 0.0, left) + jnp.where(first, 0.0, right)
            from_low[h, core] = jnp.where(first, pltpu.roll(edges[h], 48 - 16 * core, 1) + right, 0.0)
            from_high[h, core] = jnp.where(last, pltpu.roll(edges[h], 32 - 16 * core, 1) + left, 0.0)
    above = jnp.where(part >= 4, pltpu.roll(from_low[1, 1], 4, 0), 0.0)
    below = jnp.where(part < 12, pltpu.roll(from_high[0, 0], 12, 0), 0.0)
    sums = {
        (0, 0): above + from_high[0, 1],
        (0, 1): from_low[0, 0] + from_high[1, 0],
        (1, 0): from_low[0, 1] + from_high[1, 1],
        (1, 1): from_low[1, 0] + below,
    }
    rest = edges[0] + edges[1]
    small = lax.broadcasted_iota(jnp.int32, (8, I), 1)
    low = lax.broadcasted_iota(jnp.int32, (8, I), 0) < 4
    rest = jnp.where(small < 112, pltpu.roll(swap_rows(rest[:8]), I - 16, 1), rest[:8])
    for core in range(2):
        rows = slice(16 * core, 16 * core + 16)
        main = [sum(p[rows] for p in parts[8 * h : 8 * h + 8]) for h in range(2)]
        total = jnp.where(
            z_hi == 0, main[0] + body[0, core] + sums[0, core], main[1] + body[1, core] + sums[1, core]
        )
        for y in range(4):
            tile = total[8 * (y // 2) : 8 * (y // 2) + 8]
            tile = jnp.where(low, tile if y % 2 == 0 else swap_rows(tile), rest)
            message = jnp.concatenate([weights, tile], axis=0).astype(BF16)
            for x in range(4):
                out[16 * core + 4 * y + x] = message


def unpack_kernel(got, gk, ge):
    parts = [got[t].astype(F32) for t in range(32)]
    main = jnp.concatenate([p[:8] for p in parts], axis=0) * (1.0 / (ROWS * I))
    low = lax.broadcasted_iota(jnp.int32, (8, I), 0) < 4
    pairs = list(zip(parts[::2], parts[1::2]))
    rest = jnp.concatenate([jnp.where(low, swap_rows(p[8:]), q[8:]) for p, q in pairs], axis=0)
    sums = jnp.concatenate([jnp.where(low, p[8:], swap_rows(q[8:])) for p, q in pairs], axis=0)
    rest = rest * (1.0 / (ROWS * I))
    ge[...] = sums.T * float(ROWS * I) ** (-0.5)
    tail = main[192:]
    for a in range(3):
        rows = slice(C * a, C * a + C)
        gk[3 * a] = main[rows, :C]
        gk[3 * a + 1] = main[rows, C:]
        if a == 2:
            gk[3 * a + 2] = tail[:, :C]
        else:
            gk[3 * a + 2] = jnp.concatenate([rest[rows, 96:], tail[:, 64 + 32 * a : 96 + 32 * a]], axis=1)


def small_call(kernel, out_shape, ids, name, **options):
    return pl.pallas_call(
        kernel,
        out_shape=out_shape,
        in_specs=[VMEM] + [SMEM] * ids,
        out_specs=jax.tree.map(lambda _: VMEM, out_shape),
        compiler_params=pltpu.CompilerParams(vmem_limit_bytes=6 * 2**20),
        cost_estimate=pl.CostEstimate(flops=1_000_000, bytes_accessed=500_000, transcendentals=0),
        name=name,
        **options,
    )


def reduce_all(parts, ids, prediction, **options):
    got = exchange(parts, PLANE_GROUPS)
    share = small_call(share_kernel, whole((16, 56, I), BF16), 0, "plane_sums", **options)(got)
    got = exchange(share, LINE_GROUPS)
    done = small_call(finish_kernel, whole((32, 16, I), BF16), 1, "line_sums", **options)(got, ids)
    done, prediction = lax.optimization_barrier((done, prediction))
    got = exchange(done, PLANE_GROUPS)
    shapes = (whole((9, C, C), F32), whole((2 * C, I), F32))
    gk, ge = small_call(unpack_kernel, shapes, 0, "unpack", **options)(got)
    return prediction, gk, ge


def on_device(embedding, kernel, cotangent):
    rows_local = embedding.shape[0]
    row_id = lax.axis_index("row")
    col_id = lax.axis_index("col")
    place = (col_id % 8 + sum(jnp.where(row_id % 4 == n, turn, 0) for n, turn in enumerate(TURN))) % 8
    mine = lax.dynamic_slice_in_dim(embedding, place // 2 % 2 * (J - G), J + G, 0)
    window = lax.ppermute(mine, ("row", "col"), window_pairs())
    ends = jnp.concatenate([embedding[:G], embedding[rows_local - G :]], axis=0)
    ends = exchange(jnp.broadcast_to(ends[None], (ROWS,) + ends.shape), ROW_GROUPS)
    ids = jnp.stack([row_id, col_id])
    cot = cotangent.transpose(1, 2, 0)
    ga, gae = run_back(cot, kernel.reshape(9, C, C))
    parts, act, edge = run_main(cot, ga, gae, embedding, ends, window, ids)
    taps = kernel.transpose(1, 3, 0, 2).reshape(192, 192)
    prediction, gk, ge = reduce_all(parts, ids, run_forward(act, edge, taps))
    return prediction.transpose(2, 0, 1), gk.reshape(kernel.shape), ge


def solution(mesh):
    in_specs = (P("row", None), P(), P("row", "col", None))
    out_specs = (P("row", "col", None), P(), P("row", None))
    return jax.shard_map(
        on_device, mesh=mesh, in_specs=in_specs, out_specs=out_specs, check_vma=False
    )
```
